512 devices in a mesh: ctx: 64 (over y, z_hi, x, core), tp: 8 (over z_lo).
Axes of the slice: x: 4, y: 4, z: 16 (z_hi: 2, z_lo: 8; z = z_hi * 8 + z_lo), core: 2. Of those that a mesh axis runs over, the one named last changes fastest.
Arguments:
- queries: bfloat16 [32768, 3584], P('ctx', 'tp'), may hold values from -4.5 to 4.5
- keys: bfloat16 [32768, 3584], P('ctx', 'tp'), may hold values from -4.5 to 4.5
- values: bfloat16 [32768, 3584], P('ctx', 'tp'), may hold values from -6 to 6
- out_weight: bfloat16 [3584, 3584], P('tp'), may hold values from -0.125 to 0.125
- doc_lengths: int32 [32], replicated, may hold values from 1 to 2048, 32768 in all
Outputs:
- projected: bfloat16 [32768, 3584], P('ctx', 'tp')
The draws below stay inside these ranges and needn't reach their ends.
Inputs may be any that keep to these rules, and one draw needn't show every extreme that they name: `doc_lengths`: the lengths sum to 32768; the longest document has exactly 2048 tokens.
All inputs are finite; a program needn't handle non-finite values.
Results may differ from the reference program's by a relative error of at most 0.017.
Values may be sent and summed in bfloat16 or wider, within the bound.
A program may use at most 64 MiB of HBM per device.

```python
import math
import jax
import jax.numpy as jnp
import numpy as np
from jax import lax

HEADS = 32
HD = 112
D = 3584
TOKENS = 32768
DOCS = 32
DOC_MOST = 2048
N_TP = 8


def draw_queries(key, part):
    col_width = HEADS * HD
    key = jax.random.fold_in(key, 11)
    drawn = jnp.clip(jax.random.normal(key, (TOKENS, col_width), jnp.float32), -4.5, 4.5)
    return drawn.astype(jnp.bfloat16)


def draw_keys(key, part):
    col_width = HEADS * HD
    key = jax.random.fold_in(key, 12)
    drawn = jnp.clip(jax.random.normal(key, (TOKENS, col_width), jnp.float32), -4.5, 4.5)
    return drawn.astype(jnp.bfloat16)


def spiked(values, own_key, source, target, blocks, factor):
    def block_of(axis_at):
        return (jnp.arange(values.shape[axis_at]) // (values.shape[axis_at] // blocks)).reshape((-1,) + (1,) * (values.ndim - 1 - axis_at))

    first = jax.random.permutation(own_key, blocks)[block_of(target)]
    far = (block_of(target) + blocks // 2) % blocks
    return jnp.where((block_of(source) == first) | (block_of(source) == far), factor * values, values)


def block_levels(stream_key, shape, cuts, low, high):
    factor_of, own = 1.0, jax.random.fold_in(stream_key, 6)
    for position, parts in cuts:
        heights = jnp.exp(jax.random.uniform(jax.random.fold_in(own, position), (parts,), jnp.float32, low / len(cuts), high / len(cuts)))
        factor_of = factor_of * jnp.repeat(heights, shape[position] // parts).reshape([-1 if axis == position else 1 for axis in range(len(shape))])
    return factor_of


def profile(count, total, bound, slope):
    loads = [(1 << 20) // math.isqrt(rank ** slope) + 1 for rank in range(2, count + 1)]
    surplus, holding = total - bound - (count - 1), [1] * (count - 1)
    while surplus > 0:
        candidates = [i for i in range(count - 1) if holding[i] < bound]
        mass, budget = sum([loads[i] for i in candidates]), surplus
        for i in candidates:
            more = min(bound - holding[i], max(1, budget * loads[i] // mass), surplus)
            holding[i] = holding[i] + more
            surplus = surplus - more
    return np.array([bound] + holding)


def uneven(own_key, count, total, most, lean):
    if count == 2:
        one = jax.random.randint(own_key, (), max(1, total - most), min(most, total - 1) + 1)
        return jnp.stack([one, total - one])
    lengths = jnp.asarray(profile(count, total, most, lean), jnp.int32)
    pairs = (count - 1) // 2
    donor, sink = lengths[1:1 + 2 * pairs:2], lengths[2:2 + 2 * pairs:2]
    slack = jnp.minimum(donor - 1, most - sink)
    moved = jax.random.randint(jax.random.fold_in(own_key, 1), (pairs,), 0, 1 << 20) % (slack + 1)
    lengths = lengths.at[1:1 + 2 * pairs:2].set(donor - moved).at[2:2 + 2 * pairs:2].set(sink + moved)
    return lengths[jax.random.permutation(jax.random.fold_in(own_key, 2), count)]


def centred(key, shape, deviation, most, shards=(), kind=jnp.bfloat16):
    level = block_levels(key, shape, shards, -0.22, 0.18) if shards else 1.0
    result = jax.random.normal(key, shape, jnp.float32) * deviation * level
    return jnp.minimum(jnp.maximum(result, -most), most).astype(kind)


def noise_with(own_key, shape, spread, limit, shards, heavy, kind=jnp.bfloat16):
    entries = spread * jax.random.normal(own_key, shape, jnp.float32)
    if shards:
        entries = entries * block_levels(own_key, shape, shards, -0.22, 0.18)
    return jnp.clip(spiked(entries, jax.random.fold_in(own_key, 3), *heavy), -limit, limit).astype(kind)


def setup_inputs(seed: int = 0) -> dict:
    streams_of = jax.random.split(jax.random.key(seed), 6)
    return {
        "queries": draw_queries(jax.random.fold_in(streams_of[5], 71), 0),
        "keys": draw_keys(jax.random.fold_in(streams_of[5], 71), 0),
        "values": centred(streams_of[2], (TOKENS, HEADS * HD), 1.0, 6.0, ((0, 64), (1, 8))),
        "out_weight": noise_with(streams_of[3], (HEADS * HD, D), (HEADS * HD) ** -0.5, 0.125, ((0, 8),), (0, 1, 8, 2.0)),
        "doc_lengths": uneven(streams_of[4], DOCS, TOKENS, DOC_MOST, 2).astype(jnp.int32),
    }


def doc_of(positions, doc_ends):
    return lax.optimization_barrier(jnp.sum((positions[:, None] >= doc_ends[None, :]).astype(jnp.int32), axis=1))

def reference(queries, keys, values, out_weight, doc_lengths):
    col_width = HEADS * HD
    doc_ends = jnp.cumsum(doc_lengths).astype(jnp.int32)
    slopes = 2.0 ** (-4.0 * (jnp.arange(HEADS, dtype=jnp.float32) + 1.0 + HEADS) / HEADS)
    row_block = math.gcd(TOKENS, 256)
    window = min(TOKENS, row_block + DOC_MOST)

    def attend_rows(begin_at):
        key_start = jnp.clip(begin_at + row_block - window, 0, TOKENS - window).astype(jnp.int32)
        key_pos = key_start + jnp.arange(window, dtype=jnp.int32)
        key_heads = lax.dynamic_slice_in_dim(keys, key_start, window, 0).reshape(window, HEADS, HD).astype(jnp.float32)
        value_heads = lax.dynamic_slice_in_dim(values, key_start, window, 0).reshape(window, HEADS, HD).astype(jnp.float32)
        query_block = lax.dynamic_slice_in_dim(queries, begin_at, row_block, 0)
        query_heads = query_block.reshape(row_block, HEADS, HD).astype(jnp.float32)
        query_pos = begin_at + jnp.arange(row_block, dtype=jnp.int32)
        distance = (query_pos[:, None] - key_pos[None, :]).astype(jnp.float32)
        scores = jnp.einsum('qhd,khd->hqk', query_heads, key_heads) / math.sqrt(HD)
        scores = scores - slopes[:, None, None] * distance[None, :, :]
        allowed = (key_pos[None, :] <= query_pos[:, None]) & (doc_of(query_pos, doc_ends)[:, None] == doc_of(key_pos, doc_ends)[None, :])
        scores = jnp.where(allowed[None], scores, -jnp.inf)
        row_max = lax.optimization_barrier(jnp.max(scores, axis=2))
        weights = jnp.where(allowed[None], jnp.exp(scores - row_max[:, :, None]), 0.0)
        denominators = lax.optimization_barrier(jnp.sum(weights, axis=2))
        rounded = lax.optimization_barrier(weights.astype(jnp.bfloat16)).astype(jnp.float32)
        summed = jnp.einsum('hqk,khd->qhd', rounded, value_heads)
        attended = summed / jnp.transpose(denominators)[:, :, None]
        return attended.reshape(row_block, col_width).astype(jnp.bfloat16)
    starts = jnp.arange(0, TOKENS, row_block, dtype=jnp.int32)
    attended = lax.map(attend_rows, starts).reshape(TOKENS, col_width)
    group_width = col_width // N_TP

    def add_group(group, running):
        columns = lax.dynamic_slice_in_dim(attended, group * group_width, group_width, 1)
        weight_rows = lax.dynamic_slice_in_dim(out_weight, group * group_width, group_width, 0)
        partial_value = jnp.dot(columns, weight_rows, preferred_element_type=jnp.float32)
        partial_value = lax.optimization_barrier(partial_value.astype(jnp.bfloat16)).astype(jnp.float32)
        return running + partial_value
    total = lax.fori_loop(0, N_TP, add_group, jnp.zeros((TOKENS, D), jnp.float32))
    return total.astype(jnp.bfloat16)
```

```python
import functools
import math

import jax
import jax.numpy as jnp
import numpy as np
from jax import lax
from jax.experimental import pallas as pl
from jax.experimental.pallas import tpu as pltpu
from jax.sharding import PartitionSpec as P

HD = 112
EXTRA = 16
MESH = pl.DeviceIdType.MESH
LOG2E = math.log2(math.e)
NEVER = -1e30
N1, N2, N3, N4, PASS = range(5)
OWN_A, OWN_B, PASSED, SECOND, SIB_OWN, SIB_N2, SIB_N4 = range(7)


def slope_table(all_heads):
    heads = np.arange(all_heads, dtype=np.float64)
    whole = (2.0 ** (-4.0 * (heads + 1.0 + all_heads) / all_heads) * LOG2E).astype(np.float32)
    rest, terms = whole.copy(), []
    for _ in range(3):
        term = rest.astype(jnp.bfloat16).astype(np.float32)
        terms.append(term)
        rest = rest - term
    return np.stack([whole, *terms], axis=1).reshape(-1)


def attend_kernel(
    docs_ref, slopes_ref, q_ref, k_ref, v_ref, o_ref, slot, qx, scores, probs, acc, top, total, send, recv
):
    cols, rows = q_ref.shape
    head_count = cols // HD
    ctx, tp = lax.axis_index("ctx"), lax.axis_index("tp")
    last_seg = lax.axis_size("ctx") // 8 - 1
    seg, x, core = lax.div(ctx, 8), lax.rem(lax.div(ctx, 2), 4), lax.rem(ctx, 2)
    has_next, has_prev = seg < last_seg, seg > 0
    first_pos = ctx * rows

    def at(seg_of, x_of, core_of):
        return (seg_of * 8 + x_of * 2 + core_of, tp)

    sibling = at(seg, x, 1 - core)
    passes = ((x == 0) & (core == 1) | (x == 1) & (core == 0)) & has_next
    ends = x == 3
    a_does = jnp.logical_not(ends) | has_next
    a_seg = jnp.where(ends & (core == 0), seg + 1, seg)
    a_dst = at(a_seg, jnp.where(ends, 0, x + 1), core)
    a_slot = jnp.where(ends & (core == 1), PASS, N2)
    b_does = (x < 2) | (x == 2) & has_next
    b_seg = jnp.where((x == 2) & (core == 1), seg + 1, seg)
    b_dst = at(b_seg, jnp.where(x < 2, x + 2, jnp.where(core == 1, 0, 1)), core)
    b_slot = jnp.where((x == 2) & (core == 0), PASS, N4)
    p_dst = at(seg + 1, 0, core)
    p_slot = jnp.where(core == 1, N2, N4)
    second = (x == 0) & has_prev

    barrier = pltpu.get_barrier_semaphore()

    def greet(condition, device):
        @pl.when(condition)
        def _():
            pl.semaphore_signal(barrier, inc=1, device_id=device, device_id_type=MESH)

    pl.semaphore_signal(barrier, inc=1, device_id=sibling, device_id_type=MESH)
    greet((x > 0), at(seg, x - 1, core))
    greet(second & (core == 0), at(seg - 1, 3, 0))
    greet(second & (core == 1), at(seg - 1, 0, 1))
    greet(x > 1, at(seg, x - 2, core))
    greet((x == 1) & has_prev, at(seg, 0, core))
    greet(second & (core == 1), at(seg - 1, 2, 1))
    greet(second & (core == 0), at(seg - 1, 1, 0))
    greet((x == 0) & (core == 1) & has_next, at(seg, 3, 1))
    greet((x == 1) & (core == 0) & has_next, at(seg, 2, 0))
    awaited = 1 + a_does.astype(jnp.int32) + b_does.astype(jnp.int32)
    awaited = awaited + passes.astype(jnp.int32) + second.astype(jnp.int32)
    pl.semaphore_wait(barrier, awaited)

    def part(ref, head):
        return ref.at[pl.ds(pl.multiple_of(head * HD, 16), HD)]

    def copy(what, src, number, head, kv, device):
        return pltpu.make_async_remote_copy(
            src_ref=part(src, head),
            dst_ref=part(slot.at[number, kv], head),
            send_sem=send.at[what, kv, head],
            recv_sem=recv.at[number, kv, head],
            device_id=device,
            device_id_type=MESH,
        )

    def arrived(number, head, kv):
        copy(SIB_OWN, slot.at[number, kv], number, head, kv, sibling).wait_recv()

    def send_own(head, carry):
        for kv, ref in enumerate((k_ref, v_ref)):

            @pl.when(b_does & (x == 2))
            def _():
                copy(OWN_B, ref, b_slot, head, kv, b_dst).start()

            @pl.when(a_does)
            def _():
                copy(OWN_A, ref, a_slot, head, kv, a_dst).start()

            @pl.when(b_does & (x < 2))
            def _():
                copy(OWN_B, ref, b_slot, head, kv, b_dst).start()

            @pl.when(core == 0)
            def _():
                copy(SIB_OWN, ref, N1, head, kv, sibling).start()

        return carry

    lax.fori_loop(0, head_count, send_own, 0)

    for number in range(4):

        @pl.when(ctx < number + 1)
        def _():
            slot[number] = jnp.zeros(slot.shape[1:], slot.dtype)

    query_at = lax.broadcasted_iota(jnp.int32, (1, rows), 1)
    start = jnp.zeros((1, rows), jnp.int32)
    end = 0
    for doc in range(docs_ref.shape[0]):
        end = end + docs_ref[doc]
        start = jnp.where(end <= query_at + first_pos, end, start)
    start = start - first_pos
    key_at = lax.broadcasted_iota(jnp.int32, (rows, rows), 0)

    extra_row = lax.broadcasted_iota(jnp.int32, (EXTRA, rows), 0)
    extra_col = lax.broadcasted_iota(jnp.int32, (EXTRA, rows), 1)

    def key_rows(number):
        low = lax.rem(extra_col, 16)
        high = extra_col - low - (number + 1) * rows
        ones = jnp.where(extra_row < 9, 1, 0)
        picked = jnp.where(extra_row < 3, high, jnp.where(extra_row < 6, low, ones))
        return picked.astype(jnp.float32).astype(jnp.bfloat16)

    def prepare(head, carry):
        base = (tp * head_count + head) * 4
        whole = slopes_ref[base]
        here = part(q_ref, head)[...].astype(jnp.float32) * (LOG2E / math.sqrt(HD))
        high = here.astype(jnp.bfloat16)
        low = (here - high.astype(jnp.float32)).astype(jnp.bfloat16)
        shift = -whole * extra_col.astype(jnp.float32)
        shift_1 = shift.astype(jnp.bfloat16).astype(jnp.float32)
        shift_2 = (shift - shift_1).astype(jnp.bfloat16).astype(jnp.float32)
        shift_3 = shift - shift_1 - shift_2
        which = lax.rem(extra_row, 3)
        slope = jnp.where(
            which == 0, slopes_ref[base + 1], jnp.where(which == 1, slopes_ref[base + 2], slopes_ref[base + 3])
        )
        moved = jnp.where(which == 0, shift_1, jnp.where(which == 1, shift_2, shift_3))
        rows_of = jnp.where(extra_row < 6, slope, jnp.where(extra_row < 9, moved, 0.0))
        qx[head, pl.ds(0, HD)] = high
        qx[head, pl.ds(HD, EXTRA)] = rows_of.astype(jnp.bfloat16)
        qx[head, pl.ds(HD + EXTRA, HD)] = low
        qx[head, pl.ds(2 * HD + EXTRA, EXTRA)] = jnp.zeros((EXTRA, rows), jnp.bfloat16)
        return carry

    lax.fori_loop(0, head_count, prepare, 0)

    def score(keys, number, head):
        keys = jnp.concatenate([keys, key_rows(number)], axis=0)
        keys = jnp.transpose(keys)
        keys = jnp.concatenate([keys, keys], axis=1)
        return jnp.dot(keys, qx[head], preferred_element_type=jnp.float32)

    def own_block(head, carry):
        for kv in range(2):

            @pl.when(passes)
            def _():
                arrived(PASS, head, kv)
                copy(PASSED, slot.at[PASS, kv], p_slot, head, kv, p_dst).start()

        found = score(part(k_ref, head)[...], -1, head)
        allowed = (key_at <= query_at) & (key_at >= start)
        found = jnp.where(allowed, found, NEVER)
        most = jnp.max(found, axis=0, keepdims=True)
        weights = jnp.exp2(found - most)
        total[head] = jnp.sum(weights, axis=0, keepdims=True)
        top[head] = most
        part(acc, head)[...] = jnp.dot(
            part(v_ref, head)[...], weights.astype(jnp.bfloat16), preferred_element_type=jnp.float32
        )
        return carry

    lax.fori_loop(0, head_count, own_block, 0)

    def bring(head, kv):
        @pl.when(ctx >= 2)
        def _():
            arrived(N2, head, kv)
            copy(SIB_N2, slot.at[N2, kv], jnp.where(core == 0, N3, N1), head, kv, sibling).start()

        @pl.when(second)
        def _():
            copy(SECOND, slot.at[N2, kv], N4, head, kv, at(seg, 1, core)).start()

        @pl.when(ctx >= 4)
        def _():
            arrived(N4, head, kv)

        @pl.when((ctx >= 4) & (core == 1))
        def _():
            copy(SIB_N4, slot.at[N4, kv], N3, head, kv, sibling).start()

        @pl.when(ctx >= 1)
        def _():
            arrived(N1, head, kv)

        @pl.when(ctx >= 3)
        def _():
            arrived(N3, head, kv)

    def earlier_blocks(head, carry):
        bring(head, 0)
        most = top[head]
        for number in range(4):
            found = score(part(slot.at[number, 0], head)[...], number, head)
            found = jnp.where(key_at >= start + (number + 1) * rows, found, NEVER)
            scores[number] = found
            most = jnp.maximum(most, jnp.max(found, axis=0, keepdims=True))
        factor = jnp.exp2(top[head] - most)
        added = total[head] * factor
        for number in range(4):
            weights = jnp.exp2(scores[number] - most)
            added = added + jnp.sum(weights, axis=0, keepdims=True)
            probs[number] = weights.astype(jnp.bfloat16)
        bring(head, 1)
        summed = part(acc, head)[...] * factor
        for number in range(4):
            summed = summed + jnp.dot(
                part(slot.at[number, 1], head)[...], probs[number], preferred_element_type=jnp.float32
            )
        part(o_ref, head)[...] = (summed / added).astype(jnp.bfloat16)
        return carry

    lax.fori_loop(0, head_count, earlier_blocks, 0)

    def sent(head, carry):
        for kv, ref in enumerate((k_ref, v_ref)):
            for what, does in (
                (OWN_A, a_does),
                (OWN_B, b_does),
                (PASSED, passes),
                (SECOND, second),
                (SIB_OWN, core == 0),
                (SIB_N2, ctx >= 2),
                (SIB_N4, (ctx >= 4) & (core == 1)),
            ):

                @pl.when(does)
                def _():
                    copy(what, ref, N1, head, kv, sibling).wait_send()

        return carry

    lax.fori_loop(0, head_count, sent, 0)


def attend(doc_lengths, slopes, queries, keys, values):
    cols, rows = queries.shape
    heads = cols // HD
    bf16, f32 = jnp.bfloat16, jnp.float32
    vmem, smem = pl.BlockSpec(memory_space=pltpu.VMEM), pl.BlockSpec(memory_space=pltpu.SMEM)
    return pl.pallas_call(
        attend_kernel,
        out_shape=jax.ShapeDtypeStruct((cols, rows), bf16),
        in_specs=[smem, smem, vmem, vmem, vmem],
        out_specs=vmem,
        scratch_shapes=[
            pltpu.VMEM((5, 2, cols, rows), bf16),
            pltpu.VMEM((heads, 2 * (HD + EXTRA), rows), bf16),
            pltpu.VMEM((4, rows, rows), f32),
            pltpu.VMEM((4, rows, rows), bf16),
            pltpu.VMEM((cols, rows), f32),
            pltpu.VMEM((heads, 1, rows), f32),
            pltpu.VMEM((heads, 1, rows), f32),
            pltpu.SemaphoreType.DMA((7, 2, heads)),
            pltpu.SemaphoreType.DMA((5, 2, heads)),
        ],
        compiler_params=pltpu.CompilerParams(
            collective_id=0, has_side_effects=True, vmem_limit_bytes=48 << 20
        ),
    )(doc_lengths, slopes, queries, keys, values)


def project_kernel(w_ref, a_ref, o_ref, part, came, send, recv):
    cols, rows = a_ref.shape
    half = rows // 2
    n = part.shape[0]
    ctx, me = lax.axis_index("ctx"), lax.axis_index("tp")
    up, down = (ctx, me + 1), (ctx, me - 1)

    barrier = pltpu.get_barrier_semaphore()

    @pl.when(me > 0)
    def _():
        pl.semaphore_signal(barrier, inc=1, device_id=down, device_id_type=MESH)

    @pl.when(me < n - 1)
    def _():
        pl.semaphore_signal(barrier, inc=1, device_id=up, device_id_type=MESH)

    pl.semaphore_wait(barrier, (me > 0).astype(jnp.int32) + (me < n - 1).astype(jnp.int32))

    def copy(way, owner, piece):
        return pltpu.make_async_remote_copy(
            src_ref=part.at[owner, piece],
            dst_ref=came.at[way, owner, piece],
            send_sem=send.at[owner, piece],
            recv_sem=recv.at[way, owner, piece],
            device_id=up if way == 0 else down,
            device_id_type=MESH,
        )

    def multiply(step, carry):
        pair = jnp.where(me < n // 2, n // 2 - 1 - step, step)
        columns = pl.ds(pl.multiple_of(pair * 2 * cols, 128), 2 * cols)
        found = lax.dot_general(
            w_ref[:, columns], a_ref[...], (((0,), (0,)), ((), ())), preferred_element_type=jnp.float32
        ).astype(jnp.bfloat16)
        for number in range(2):
            for piece in range(2):
                part[2 * pair + number, piece] = found[
                    number * cols : (number + 1) * cols, piece * half : (piece + 1) * half
                ]
        for number in range(2):
            for piece in range(2):

                @pl.when((me == 0) & (2 * pair + 1 - number > 0))
                def _():
                    copy(0, 2 * pair + 1 - number, piece).start()

                @pl.when((me == n - 1) & (2 * pair + number < n - 1))
                def _():
                    copy(1, 2 * pair + number, piece).start()

        return carry

    lax.fori_loop(0, n // 2, multiply, 0)

    def pass_on(way, owner, piece):
        copy(way, owner, piece).wait_recv()
        summed = part[owner, piece].astype(jnp.float32) + came[way, owner, piece].astype(jnp.float32)
        part[owner, piece] = summed.astype(jnp.bfloat16)
        copy(way, owner, piece).start()

    inner = (me > 0) & (me < n - 1)

    def relay(step, carry):
        unit = step - me
        owner = n - 1 - lax.div(unit, 2)

        @pl.when(inner & (unit >= 0) & (owner > me))
        def _():
            pass_on(0, owner, lax.rem(unit, 2))

        unit_down = step - (n - 1 - me)
        owner_down = lax.div(unit_down, 2)

        @pl.when(inner & (unit_down >= 0) & (owner_down < me))
        def _():
            pass_on(1, owner_down, lax.rem(unit_down, 2))

        return carry

    lax.fori_loop(0, 2 * n - 3, relay, 0)

    for piece in range(2):

        @pl.when(me > 0)
        def _():
            copy(0, me, piece).wait_recv()

        @pl.when(me < n - 1)
        def _():
            copy(1, me, piece).wait_recv()

        own = part[me, piece].astype(jnp.float32)
        below = jnp.where(me > 0, came[0, me, piece].astype(jnp.float32), 0.0)
        above = jnp.where(me < n - 1, came[1, me, piece].astype(jnp.float32), 0.0)
        o_ref[:, piece * half : (piece + 1) * half] = (own + below + above).astype(jnp.bfloat16)

    def sent(owner, carry):
        for piece in range(2):

            @pl.when(owner != me)
            def _():
                copy(0, owner, piece).wait_send()

        return carry

    lax.fori_loop(0, n, sent, 0)


def project(out_weight, attended):
    cols, rows = attended.shape
    n = out_weight.shape[1] // cols
    bf16 = jnp.bfloat16
    vmem = pl.BlockSpec(memory_space=pltpu.VMEM)
    return pl.pallas_call(
        project_kernel,
        out_shape=jax.ShapeDtypeStruct((cols, rows), bf16),
        in_specs=[vmem, vmem],
        out_specs=vmem,
        scratch_shapes=[
            pltpu.VMEM((n, 2, cols, rows // 2), bf16),
            pltpu.VMEM((2, n, 2, cols, rows // 2), bf16),
            pltpu.SemaphoreType.DMA((n, 2)),
            pltpu.SemaphoreType.DMA((2, n, 2)),
        ],
        compiler_params=pltpu.CompilerParams(
            collective_id=1, has_side_effects=True, vmem_limit_bytes=48 << 20
        ),
    )(out_weight, attended)


def body(queries, keys, values, out_weight, doc_lengths):
    all_heads = queries.shape[1] // HD * lax.axis_size("tp")
    slopes = jnp.asarray(slope_table(all_heads))
    attended = attend(doc_lengths, slopes, queries.T, keys.T, values.T)
    return project(out_weight, attended).T


def solution(mesh):
    placed = (P("ctx", "tp"), P("ctx", "tp"), P("ctx", "tp"), P("tp", None), P())
    return jax.shard_map(
        body, mesh=mesh, in_specs=placed, out_specs=P("ctx", "tp"), check_vma=False
    )
```

```python
import functools
import math

import jax
import jax.numpy as jnp
import numpy as np
from jax import lax
from jax.experimental import pallas as pl
from jax.experimental.pallas import tpu as pltpu
from jax.sharding import PartitionSpec as P

HD = 112
EXTRA = 16
MESH = pl.DeviceIdType.MESH
LOG2E = math.log2(math.e)
NEVER = -1e30
N1, N2, N3, N4, PASS = range(5)
OWN_A, OWN_B, PASSED, SECOND, SIB_OWN, SIB_N2, SIB_N4 = range(7)
UP, DOWN = range(2)
PIECES = 4


def slope_table(all_heads):
    heads = np.arange(all_heads, dtype=np.float64)
    whole = (2.0 ** (-4.0 * (heads + 1.0 + all_heads) / all_heads) * LOG2E).astype(np.float32)
    rest, terms = whole.copy(), []
    for _ in range(3):
        term = rest.astype(jnp.bfloat16).astype(np.float32)
        terms.append(term)
        rest = rest - term
    return np.stack([whole, *terms], axis=1).reshape(-1)


def weight_rows(cols, y_count):
    return 16 * -(-cols // (16 * 8 * y_count))


def layer_kernel(
    docs_ref, slopes_ref, q_hbm, k_hbm, v_hbm, w_hbm, o_ref,
    q_ref, own, w_ref, slot, qx, scores, probs, acc, top, total,
    wt, wc, first_half, spread, part, came, second_half,
    load, send, recv, z_send, z_recv, x_send, y_send, c_send, w_recv, spread_send, spread_recv, part_send, part_recv, go,
):
    cols, rows = q_ref.shape
    head_count = cols // HD
    n = wt.shape[0]
    piece_len = rows // PIECES
    ctx, me = lax.axis_index("ctx"), lax.axis_index("tp")
    segs = lax.axis_size("ctx") // 8
    y_count = max(1, segs // 2)
    w_rows = weight_rows(cols, y_count)
    seg, x, core = lax.div(ctx, 8), lax.rem(lax.div(ctx, 2), 4), lax.rem(ctx, 2)
    y = lax.div(ctx, 16)
    has_next, has_prev = seg < segs - 1, seg > 0
    first_pos = ctx * rows

    def at(seg_of, x_of, core_of):
        return (seg_of * 8 + x_of * 2 + core_of, me)

    sibling = at(seg, x, 1 - core)
    crosses_a = (x == 3) & (core == 0) & has_next
    crosses_b = (x == 2) & (core == 1) & has_next
    passes = ((x == 0) & (core == 1) | (x == 1) & (core == 0)) & has_next
    ends = x == 3
    a_does = jnp.logical_not(ends) | has_next
    a_seg = jnp.where(ends & (core == 0), seg + 1, seg)
    a_dst = at(a_seg, jnp.where(ends, 0, x + 1), core)
    a_slot = jnp.where(ends & (core == 1), PASS, N2)
    b_does = (x < 2) | (x == 2) & has_next
    b_seg = jnp.where((x == 2) & (core == 1), seg + 1, seg)
    b_dst = at(b_seg, jnp.where(x < 2, x + 2, jnp.where(core == 1, 0, 1)), core)
    b_slot = jnp.where((x == 2) & (core == 0), PASS, N4)
    p_dst = at(seg + 1, 0, core)
    p_slot = jnp.where(core == 1, N2, N4)
    second = (x == 0) & has_prev
    gives = (x == 0) & has_prev
    gives_first = (x == 0) & (seg == 1)
    held = (x >= 2) & has_prev
    if segs > 1:
        held = held | (seg == 0)

    barrier = pltpu.get_barrier_semaphore()

    def greet(condition, device):
        @pl.when(condition)
        def _():
            pl.semaphore_signal(barrier, inc=1, device_id=device, device_id_type=MESH)

    pl.semaphore_signal(barrier, inc=1, device_id=sibling, device_id_type=MESH)
    greet(second & (core == 0), at(seg - 1, 3, 0))
    greet(second & (core == 0), at(seg - 1, 1, 0))
    greet(second & (core == 1), at(seg - 1, 2, 1))
    greet(second & (core == 1), at(seg - 1, 0, 1))
    if segs > 1:
        greet(seg == 0, at(1, 0, core))

    def greet_x(step, carry):
        pl.semaphore_signal(barrier, inc=1, device_id=at(seg, lax.rem(x + step, 4), core), device_id_type=MESH)
        return carry

    lax.fori_loop(1, 4, greet_x, 0)

    def y_at(step):
        return (lax.rem(ctx + step * 16, y_count * 16), me)

    def greet_y(step, carry):
        pl.semaphore_signal(barrier, inc=1, device_id=y_at(step), device_id_type=MESH)
        return carry

    if y_count > 1:
        lax.fori_loop(1, y_count, greet_y, 0)

    def greet_z(step, carry):
        pl.semaphore_signal(barrier, inc=1, device_id=(ctx, lax.rem(me + step, n)), device_id_type=MESH)
        return carry

    lax.fori_loop(1, n, greet_z, 0)

    loads = [
        pltpu.make_async_copy(k_hbm, own.at[0], load.at[0]),
        pltpu.make_async_copy(v_hbm, own.at[1], load.at[1]),
        pltpu.make_async_copy(q_hbm, q_ref, load.at[2]),
        pltpu.make_async_copy(w_hbm, w_ref, load.at[3]),
    ]
    for one in loads:
        one.start()

    crossing = crosses_a.astype(jnp.int32) + crosses_b.astype(jnp.int32) + passes.astype(jnp.int32)
    awaited = 1 + 3 + (y_count - 1) + (n - 1) + crossing + 4 * gives_first.astype(jnp.int32)
    pl.semaphore_wait(barrier, awaited)

    def remote(src, dst, send_sem, recv_sem, device):
        return pltpu.make_async_remote_copy(
            src_ref=src, dst_ref=dst, send_sem=send_sem, recv_sem=recv_sem, device_id=device, device_id_type=MESH
        )

    def part_of(ref, head):
        return ref.at[pl.ds(pl.multiple_of(head * HD, 16), HD)]

    def copy(what, src, number, head, kv, device):
        return remote(
            part_of(src, head),
            part_of(slot.at[number, kv], head),
            send.at[what, kv, head],
            recv.at[number, kv, head],
            device,
        )

    def arrived(number, head, kv):
        copy(SIB_OWN, slot.at[number, kv], number, head, kv, sibling).wait_recv()

    def send_own(head, carry):
        for kv, ref in enumerate((k_hbm, v_hbm)):

            @pl.when(b_does & (x == 2))
            def _():
                copy(OWN_B, ref, b_slot, head, kv, b_dst).start()

            @pl.when(a_does)
            def _():
                copy(OWN_A, ref, a_slot, head, kv, a_dst).start()

            @pl.when(b_does & (x < 2))
            def _():
                copy(OWN_B, ref, b_slot, head, kv, b_dst).start()

            @pl.when(core == 0)
            def _():
                copy(SIB_OWN, ref, N1, head, kv, sibling).start()

        return carry

    def pass_on(head):
        for kv in range(2):

            @pl.when(passes)
            def _():
                arrived(PASS, head, kv)
                copy(PASSED, slot.at[PASS, kv], p_slot, head, kv, p_dst).start()

        @pl.when(passes)
        def _():
            send_own(head, 0)

    @pl.when(jnp.logical_not(passes))
    def _():
        lax.fori_loop(0, head_count, send_own, 0)

    for number in range(4):

        @pl.when(ctx < number + 1)
        def _():
            slot[number] = jnp.zeros(slot.shape[1:], slot.dtype)

    for one in loads:
        one.wait()

    pass_on(0)

    def transpose_pair(pair, carry):
        columns = pl.ds(pl.multiple_of(pair * 2 * cols, 128), 2 * cols)
        found = jnp.transpose(w_ref[:, columns])
        wt[2 * pair] = found[:cols]
        wt[2 * pair + 1] = found[cols:]
        return carry

    lax.fori_loop(0, n // 2, transpose_pair, 0)

    def region(y_of, x_of, core_of):
        return y_of * 8 + core_of * 4 + x_of

    def region_rows(number):
        return pl.ds(pl.multiple_of(number * w_rows, 16), w_rows)

    def there(number):
        return number * w_rows < cols

    mine = region(y, x, core)

    def z_copy(other):
        return remote(
            wt.at[other, region_rows(mine)],
            wc.at[me, region_rows(mine)],
            z_send.at[other],
            z_recv.at[me],
            (ctx, other),
        )

    def z_arrival(other):
        return remote(
            wt.at[other, region_rows(mine)],
            wc.at[other, region_rows(mine)],
            z_send.at[other],
            z_recv.at[other],
            (ctx, other),
        )

    @pl.when(there(mine))
    def _():
        wc[me, region_rows(mine)] = wt[me, region_rows(mine)]

        def start(step, carry):
            z_copy(lax.rem(me + step, n)).start()
            return carry

        lax.fori_loop(1, n, start, 0)

    def w_copy(number, send_sem, device):
        rows_of = region_rows(number)
        return remote(wc.at[:, rows_of], wc.at[:, rows_of], send_sem, w_recv.at[number], device)

    def x_stage():
        @pl.when(there(mine))
        def _():
            def wait(step, carry):
                z_arrival(lax.rem(me + step, n)).wait_recv()
                return carry

            lax.fori_loop(1, n, wait, 0)

            def start(step, carry):
                w_copy(mine, x_send.at[step], at(seg, lax.rem(x + step, 4), core)).start()
                return carry

            lax.fori_loop(1, 4, start, 0)

    def y_stage():
        def one(x_of, carry):
            number = region(y, x_of, core)

            @pl.when(there(number) & (x_of != x))
            def _():
                w_copy(number, x_send.at[0], sibling).wait_recv()

            if y_count > 1:

                @pl.when(there(number))
                def _():
                    def start(step, carry):
                        w_copy(number, y_send.at[x_of, step], y_at(step)).start()
                        return carry

                    lax.fori_loop(1, y_count, start, 0)

            return carry

        lax.fori_loop(0, 4, one, 0)

    def each_lane_region(core_of, do):
        def one(index, carry):
            y_of, x_of = lax.div(index, 4), lax.rem(index, 4)
            number = region(y_of, x_of, core_of)

            @pl.when(there(number))
            def _():
                do(number, y_of)

            return carry

        lax.fori_loop(0, 4 * y_count, one, 0)

    def c_stage():
        def hand_over(number, y_of):
            @pl.when(y_of != y)
            def _():
                w_copy(number, x_send.at[0], sibling).wait_recv()

            w_copy(number, c_send.at[number], sibling).start()

        each_lane_region(core, hand_over)

    def c_arrivals():
        def wait(number, y_of):
            w_copy(number, c_send.at[number], sibling).wait_recv()

        each_lane_region(1 - core, wait)

    def w_sent():
        @pl.when(there(mine))
        def _():
            def z_wait(step, carry):
                z_copy(lax.rem(me + step, n)).wait_send()
                return carry

            lax.fori_loop(1, n, z_wait, 0)

            def x_wait(step, carry):
                w_copy(mine, x_send.at[step], sibling).wait_send()
                return carry

            lax.fori_loop(1, 4, x_wait, 0)

        def y_wait(x_of, carry):
            number = region(y, x_of, core)

            @pl.when(there(number))
            def _():
                def wait(step, carry):
                    w_copy(number, y_send.at[x_of, step], sibling).wait_send()
                    return carry

                lax.fori_loop(1, y_count, wait, 0)

            return carry

        if y_count > 1:
            lax.fori_loop(0, 4, y_wait, 0)
        each_lane_region(core, lambda number, y_of: w_copy(number, c_send.at[number], sibling).wait_send())

    query_at = lax.broadcasted_iota(jnp.int32, (1, rows), 1)
    start = jnp.zeros((1, rows), jnp.int32)
    end = 0
    for doc in range(docs_ref.shape[0]):
        end = end + docs_ref[doc]
        start = jnp.where(end <= query_at + first_pos, end, start)
    start = start - first_pos
    key_at = lax.broadcasted_iota(jnp.int32, (rows, rows), 0)

    extra_row = lax.broadcasted_iota(jnp.int32, (EXTRA, rows), 0)
    extra_col = lax.broadcasted_iota(jnp.int32, (EXTRA, rows), 1)

    def key_rows(number):
        low = lax.rem(extra_col, 16)
        high = extra_col - low - (number + 1) * rows
        ones = jnp.where(extra_row < 9, 1, 0)
        picked = jnp.where(extra_row < 3, high, jnp.where(extra_row < 6, low, ones))
        return picked.astype(jnp.float32).astype(jnp.bfloat16)

    def prepare(head, carry):
        base = (me * head_count + head) * 4
        whole = slopes_ref[base]
        here = part_of(q_ref, head)[...].astype(jnp.float32) * (LOG2E / math.sqrt(HD))
        high = here.astype(jnp.bfloat16)
        low = (here - high.astype(jnp.float32)).astype(jnp.bfloat16)
        shift = -whole * extra_col.astype(jnp.float32)
        shift_1 = shift.astype(jnp.bfloat16).astype(jnp.float32)
        shift_2 = (shift - shift_1).astype(jnp.bfloat16).astype(jnp.float32)
        shift_3 = shift - shift_1 - shift_2
        which = lax.rem(extra_row, 3)
        slope = jnp.where(
            which == 0, slopes_ref[base + 1], jnp.where(which == 1, slopes_ref[base + 2], slopes_ref[base + 3])
        )
        moved = jnp.where(which == 0, shift_1, jnp.where(which == 1, shift_2, shift_3))
        rows_of = jnp.where(extra_row < 6, slope, jnp.where(extra_row < 9, moved, 0.0))
        qx[head, pl.ds(0, HD)] = high
        qx[head, pl.ds(HD, EXTRA)] = rows_of.astype(jnp.bfloat16)
        qx[head, pl.ds(HD + EXTRA, HD)] = low
        qx[head, pl.ds(2 * HD + EXTRA, EXTRA)] = jnp.zeros((EXTRA, rows), jnp.bfloat16)
        return carry

    lax.fori_loop(0, head_count, prepare, 0)

    def score(keys, number, head):
        keys = jnp.concatenate([keys, key_rows(number)], axis=0)
        keys = jnp.transpose(keys)
        keys = jnp.concatenate([keys, keys], axis=1)
        return jnp.dot(keys, qx[head], preferred_element_type=jnp.float32)

    def own_block(head, carry):
        @pl.when(head > 0)
        def _():
            pass_on(head)

        found = score(part_of(own.at[0], head)[...], -1, head)
        allowed = (key_at <= query_at) & (key_at >= start)
        found = jnp.where(allowed, found, NEVER)
        most = jnp.max(found, axis=0, keepdims=True)
        weights = jnp.exp2(found - most)
        total[head] = jnp.sum(weights, axis=0, keepdims=True)
        top[head] = most
        part_of(acc, head)[...] = jnp.dot(
            part_of(own.at[1], head)[...], weights.astype(jnp.bfloat16), preferred_element_type=jnp.float32
        )
        return carry

    lax.fori_loop(0, head_count, own_block, 0)
    x_stage()

    def bring(head, kv):
        @pl.when(ctx >= 2)
        def _():
            arrived(N2, head, kv)
            copy(SIB_N2, slot.at[N2, kv], jnp.where(core == 0, N3, N1), head, kv, sibling).start()

        @pl.when(second)
        def _():
            copy(SECOND, slot.at[N2, kv], N4, head, kv, at(seg, 1, core)).start()

        @pl.when(ctx >= 4)
        def _():
            arrived(N4, head, kv)

        @pl.when((ctx >= 4) & (core == 1))
        def _():
            copy(SIB_N4, slot.at[N4, kv], N3, head, kv, sibling).start()

        @pl.when(ctx >= 1)
        def _():
            arrived(N1, head, kv)

        @pl.when(ctx >= 3)
        def _():
            arrived(N3, head, kv)

    def earlier_blocks(head, carry):
        bring(head, 0)
        most = top[head]
        for number in range(4):
            found = score(part_of(slot.at[number, 0], head)[...], number, head)
            found = jnp.where(key_at >= start + (number + 1) * rows, found, NEVER)
            scores[number] = found
            most = jnp.maximum(most, jnp.max(found, axis=0, keepdims=True))
        factor = jnp.exp2(top[head] - most)
        added = total[head] * factor
        for number in range(4):
            weights = jnp.exp2(scores[number] - most)
            added = added + jnp.sum(weights, axis=0, keepdims=True)
            probs[number] = weights.astype(jnp.bfloat16)
        bring(head, 1)

        @pl.when((head == head_count - 1) & gives)
        def _():
            for x_of in (2, 3):
                pl.semaphore_signal(go, inc=1, device_id=at(seg, x_of, core), device_id_type=MESH)

        @pl.when((head == head_count - 1) & gives_first)
        def _():
            for x_of in range(4):
                pl.semaphore_signal(go, inc=1, device_id=at(0, x_of, core), device_id_type=MESH)

        summed = part_of(acc, head)[...] * factor
        for number in range(4):
            summed = summed + jnp.dot(
                part_of(slot.at[number, 1], head)[...], probs[number], preferred_element_type=jnp.float32
            )
        attended = (summed / added).astype(jnp.bfloat16)
        part_of(first_half, head)[...] = attended[:, : 2 * piece_len]
        for piece in range(2):
            part_of(spread.at[me, piece], head)[...] = attended[:, (2 + piece) * piece_len : (3 + piece) * piece_len]

        @pl.when(head == 0)
        def _():
            y_stage()

        return carry

    lax.fori_loop(0, head_count, earlier_blocks, 0)

    @pl.when(held)
    def _():
        pl.semaphore_wait(go, 1)

    places = ((ctx, me + 1), (ctx, me - 1))
    below = (me, n - 1 - me)

    def spread_copy(way, source, piece):
        ref = spread.at[source, piece]
        return remote(ref, ref, spread_send.at[way, source, piece], spread_recv.at[source, piece], places[way])

    def part_copy(way, owner, piece):
        return remote(
            part.at[owner, piece],
            came.at[way, owner, piece],
            part_send.at[owner, piece],
            part_recv.at[way, owner, piece],
            places[way],
        )

    for piece in range(2):
        for way in (UP, DOWN):

            @pl.when(below[way] < n - 1)
            def _():
                spread_copy(way, me, piece).start()

    c_stage()

    def partials(owner, carry):
        found = jnp.dot(wt[owner], first_half[...], preferred_element_type=jnp.float32).astype(jnp.bfloat16)
        for piece in range(2):
            part[owner, piece] = found[:, piece * piece_len : (piece + 1) * piece_len]
        return carry

    lax.fori_loop(0, n, partials, 0)
    for piece in range(2):
        second_half[piece] = jnp.dot(wt[me], spread[me, piece], preferred_element_type=jnp.float32)
    c_arrivals()

    def slot_of(time, carry):
        number, piece = lax.div(time, 2), lax.rem(time, 2)
        for way in (UP, DOWN):
            behind = below[way]
            sign = 1 - 2 * way
            source = me - sign * number

            @pl.when(number <= behind)
            def _():
                spread_copy(way, source, piece).wait_recv()

            @pl.when((number <= behind) & (behind < n - 1))
            def _():
                spread_copy(way, source, piece).start()

            owner = jnp.where(way == UP, n - 1, 0) - sign * (number - behind - 1)
            sums = (number > behind) & (behind < n - 1)

            @pl.when(sums & (behind > 0))
            def _():
                part_copy(way, owner, piece).wait_recv()
                summed = part[owner, piece].astype(jnp.float32) + came[way, owner, piece].astype(jnp.float32)
                part[owner, piece] = summed.astype(jnp.bfloat16)

            @pl.when(sums)
            def _():
                part_copy(way, owner, piece).start()

        for way in (UP, DOWN):
            source = me - (1 - 2 * way) * number

            @pl.when(number <= below[way])
            def _():
                second_half[piece] += jnp.dot(wc[source], spread[source, piece], preferred_element_type=jnp.float32)

        return carry

    lax.fori_loop(2, 2 * n, slot_of, 0)

    for piece in range(2):
        for way in (UP, DOWN):

            @pl.when(below[way] > 0)
            def _():
                part_copy(way, me, piece).wait_recv()

        whole = part[me, piece].astype(jnp.float32)
        for way in (UP, DOWN):
            whole = whole + jnp.where(below[way] > 0, came[way, me, piece].astype(jnp.float32), 0.0)
        o_ref[:, piece * piece_len : (piece + 1) * piece_len] = whole.astype(jnp.bfloat16)
        o_ref[:, (2 + piece) * piece_len : (3 + piece) * piece_len] = second_half[piece].astype(jnp.bfloat16)

    def sent(head, carry):
        for kv, ref in enumerate((k_hbm, v_hbm)):
            for what, does in (
                (OWN_A, a_does),
                (OWN_B, b_does),
                (PASSED, passes),
                (SECOND, second),
                (SIB_OWN, core == 0),
                (SIB_N2, ctx >= 2),
                (SIB_N4, (ctx >= 4) & (core == 1)),
            ):

                @pl.when(does)
                def _():
                    copy(what, ref, N1, head, kv, sibling).wait_send()

        return carry

    lax.fori_loop(0, head_count, sent, 0)
    w_sent()

    def sums_sent(other, carry):
        for piece in range(2):

            @pl.when(other != me)
            def _():
                part_copy(UP, other, piece).wait_send()

            for way in (UP, DOWN):
                sign = 1 - 2 * way
                passed = (below[way] < n - 1) & ((me - other) * sign >= 0)

                @pl.when(passed)
                def _():
                    spread_copy(way, other, piece).wait_send()

        return carry

    lax.fori_loop(0, n, sums_sent, 0)


def layer(doc_lengths, slopes, queries, keys, values, out_weight):
    cols, rows = queries.shape
    heads = cols // HD
    n = out_weight.shape[1] // cols
    y_count = max(1, lax.axis_size("ctx") // 16)
    regions = 8 * y_count
    piece = rows // PIECES
    bf16, f32 = jnp.bfloat16, jnp.float32
    vmem, smem = pl.BlockSpec(memory_space=pltpu.VMEM), pl.BlockSpec(memory_space=pltpu.SMEM)
    anywhere = pl.BlockSpec(memory_space=pl.ANY)
    dma = pltpu.SemaphoreType.DMA
    return pl.pallas_call(
        layer_kernel,
        out_shape=jax.ShapeDtypeStruct((cols, rows), bf16),
        in_specs=[smem, smem, anywhere, anywhere, anywhere, anywhere],
        out_specs=vmem,
        scratch_shapes=[
            pltpu.VMEM((cols, rows), bf16),
            pltpu.VMEM((2, cols, rows), bf16),
            pltpu.VMEM((cols, n * cols), bf16),
            pltpu.VMEM((5, 2, cols, rows), bf16),
            pltpu.VMEM((heads, 2 * (HD + EXTRA), rows), bf16),
            pltpu.VMEM((4, rows, rows), f32),
            pltpu.VMEM((4, rows, rows), bf16),
            pltpu.VMEM((cols, rows), f32),
            pltpu.VMEM((heads, 1, rows), f32),
            pltpu.VMEM((heads, 1, rows), f32),
            pltpu.VMEM((n, cols, cols), bf16),
            pltpu.VMEM((n, cols, cols), bf16),
            pltpu.VMEM((cols, 2 * piece), bf16),
            pltpu.VMEM((n, 2, cols, piece), bf16),
            pltpu.VMEM((n, 2, cols, piece), bf16),
            pltpu.VMEM((2, n, 2, cols, piece), bf16),
            pltpu.VMEM((2, cols, piece), f32),
            dma((4,)),
            dma((7, 2, heads)),
            dma((5, 2, heads)),
            dma((n,)),
            dma((n,)),
            dma((4,)),
            dma((4, y_count)),
            dma((regions,)),
            dma((regions,)),
            dma((2, n, 2)),
            dma((n, 2)),
            dma((n, 2)),
            dma((2, n, 2)),
            pltpu.SemaphoreType.REGULAR,
        ],
        compiler_params=pltpu.CompilerParams(
            collective_id=0, has_side_effects=True, vmem_limit_bytes=56 << 20
        ),
    )(doc_lengths, slopes, queries, keys, values, out_weight)


def body(queries, keys, values, out_weight, doc_lengths):
    all_heads = queries.shape[1] // HD * lax.axis_size("tp")
    slopes = jnp.asarray(slope_table(all_heads))
    return layer(doc_lengths, slopes, queries.T, keys.T, values.T, out_weight).T


def solution(mesh):
    placed = (P("ctx", "tp"), P("ctx", "tp"), P("ctx", "tp"), P("tp", None), P())
    return jax.shard_map(
        body, mesh=mesh, in_specs=placed, out_specs=P("ctx", "tp"), check_vma=False
    )
```

```python
import functools
import math

import jax
import jax.numpy as jnp
import numpy as np
from jax import lax
from jax.experimental import pallas as pl
from jax.experimental.pallas import tpu as pltpu
from jax.sharding import PartitionSpec as P

HD = 112
EXTRA = 16
MESH = pl.DeviceIdType.MESH
LOG2E = math.log2(math.e)
NEVER = -1e30
N1, N2, N3, N4, PASS = range(5)
OWN_A, OWN_B, CROSSES, PASSED, SECOND, SIB_OWN, SIB_N2, SIB_N4 = range(8)
UP, DOWN = range(2)
PIECES = 4


def slope_table(all_heads):
    heads = np.arange(all_heads, dtype=np.float64)
    whole = (2.0 ** (-4.0 * (heads + 1.0 + all_heads) / all_heads) * LOG2E).astype(np.float32)
    rest, terms = whole.copy(), []
    for _ in range(3):
        term = rest.astype(jnp.bfloat16).astype(np.float32)
        terms.append(term)
        rest = rest - term
    return np.stack([whole, *terms], axis=1).reshape(-1)


def weight_rows(cols, y_count):
    return 16 * -(-cols // (16 * 8 * y_count))


def layer_kernel(
    docs_ref, slopes_ref, q_hbm, k_hbm, v_hbm, w_hbm, o_ref,
    q_ref, own, w_ref, slot, qx, scores, probs, acc, top, total,
    wt, wc, first_half, spread, part, came, second_half,
    load, send, recv, z_send, z_recv, x_send, y_send, c_send, w_recv, spread_send, spread_recv, part_send, part_recv, go,
):
    cols, rows = q_ref.shape
    head_count = cols // HD
    n = wt.shape[0]
    piece_len = rows // PIECES
    ctx, me = lax.axis_index("ctx"), lax.axis_index("tp")
    segs = lax.axis_size("ctx") // 8
    y_count = max(1, segs // 2)
    w_rows = weight_rows(cols, y_count)
    seg, x, core = lax.div(ctx, 8), lax.rem(lax.div(ctx, 2), 4), lax.rem(ctx, 2)
    y = lax.div(ctx, 16)
    has_next, has_prev = seg < segs - 1, seg > 0
    first_pos = ctx * rows

    def at(seg_of, x_of, core_of):
        return (seg_of * 8 + x_of * 2 + core_of, me)

    sibling = at(seg, x, 1 - core)
    upper = lax.rem(seg, 2) == 1
    crosses = (x >= 2) & has_next
    on_column = lax.rem(x, 2) != core
    goes_round = crosses & on_column & jnp.logical_not(upper)
    pass_x = jnp.where(x == 3, jnp.where(core == 1, 0, 3), jnp.where(core == 1, 2, 1))
    x_slot = jnp.where((x == 0) | (x == 3), N2, N4)
    c_dst = at(
        jnp.where(goes_round, seg + 1, jnp.where(upper, seg + 2, seg)), jnp.where(goes_round, 0, pass_x), core
    )
    c_slot = jnp.where(goes_round, x_slot, PASS)
    passes = on_column & (jnp.where(upper, seg, 0) != 1) & (upper | (x < 2) & has_next)
    p_source = at(jnp.where(upper, seg - 2, seg), jnp.where((x == 0) | (x == 3), 3, 2), core)
    p_dst = at(jnp.where(upper, seg - 1, seg + 1), 0, core)
    a_does = x < 3
    b_does = x == 1
    second = (x == 0) & has_prev | (x == 1)
    gives = (x == 0) & has_prev
    gives_first = (x == 0) & (seg == 1)
    held = (x >= 2) & has_prev
    if segs > 1:
        held = held | (seg == 0)

    barrier = pltpu.get_barrier_semaphore()

    def greet(condition, device):
        @pl.when(condition)
        def _():
            pl.semaphore_signal(barrier, inc=1, device_id=device, device_id_type=MESH)

    pl.semaphore_signal(barrier, inc=1, device_id=sibling, device_id_type=MESH)
    if segs > 1:
        greet(passes, p_source)
        for x_of in (jnp.where(core == 1, 0, 3), jnp.where(core == 1, 2, 1)):
            greet((x == 0) & has_prev, at(jnp.where(upper, seg - 1, seg + 1), x_of, core))
        greet(seg == 0, at(1, 0, core))

    def greet_x(step, carry):
        pl.semaphore_signal(barrier, inc=1, device_id=at(seg, lax.rem(x + step, 4), core), device_id_type=MESH)
        return carry

    lax.fori_loop(1, 4, greet_x, 0)

    def y_at(step):
        return (lax.rem(ctx + step * 16, y_count * 16), me)

    def greet_y(step, carry):
        pl.semaphore_signal(barrier, inc=1, device_id=y_at(step), device_id_type=MESH)
        return carry

    if y_count > 1:
        lax.fori_loop(1, y_count, greet_y, 0)

    def greet_z(step, carry):
        pl.semaphore_signal(barrier, inc=1, device_id=(ctx, lax.rem(me + step, n)), device_id_type=MESH)
        return carry

    lax.fori_loop(1, n, greet_z, 0)

    loads = [
        pltpu.make_async_copy(k_hbm, own.at[0], load.at[0]),
        pltpu.make_async_copy(v_hbm, own.at[1], load.at[1]),
        pltpu.make_async_copy(q_hbm, q_ref, load.at[2]),
        pltpu.make_async_copy(w_hbm, w_ref, load.at[3]),
    ]
    for one in loads:
        one.start()

    crossing = crosses.astype(jnp.int32) + passes.astype(jnp.int32)
    awaited = 1 + 3 + (y_count - 1) + (n - 1) + crossing + 4 * gives_first.astype(jnp.int32)
    pl.semaphore_wait(barrier, awaited)

    def remote(src, dst, send_sem, recv_sem, device):
        return pltpu.make_async_remote_copy(
            src_ref=src, dst_ref=dst, send_sem=send_sem, recv_sem=recv_sem, device_id=device, device_id_type=MESH
        )

    def part_of(ref, head):
        return ref.at[pl.ds(pl.multiple_of(head * HD, 16), HD)]

    def copy(what, src, number, head, kv, device):
        return remote(
            part_of(src, head),
            part_of(slot.at[number, kv], head),
            send.at[what, kv, head],
            recv.at[number, kv, head],
            device,
        )

    def arrived(number, head, kv):
        copy(SIB_OWN, slot.at[number, kv], number, head, kv, sibling).wait_recv()

    def send_own(head, carry):
        for kv, ref in enumerate((k_hbm, v_hbm)):

            @pl.when(a_does)
            def _():
                copy(OWN_A, ref, N2, head, kv, at(seg, x + 1, core)).start()

            @pl.when(b_does)
            def _():
                copy(OWN_B, ref, N4, head, kv, at(seg, x + 2, core)).start()

            @pl.when(core == 0)
            def _():
                copy(SIB_OWN, ref, N1, head, kv, sibling).start()

        return carry

    def send_over(head, carry):
        for kv, ref in enumerate((k_hbm, v_hbm)):

            @pl.when(crosses)
            def _():
                copy(CROSSES, ref, c_slot, head, kv, c_dst).start()

        return carry

    def pass_on(head, carry):
        for kv in range(2):

            @pl.when(passes)
            def _():
                arrived(PASS, head, kv)
                copy(PASSED, slot.at[PASS, kv], x_slot, head, kv, p_dst).start()

        return carry

    lax.fori_loop(0, head_count, send_over, 0)
    lax.fori_loop(0, head_count, send_own, 0)
    lax.fori_loop(0, head_count, pass_on, 0)
    for number in range(4):

        @pl.when(ctx < number + 1)
        def _():
            slot[number] = jnp.zeros(slot.shape[1:], slot.dtype)

    for one in loads:
        one.wait()

    def transpose_pair(pair, carry):
        columns = pl.ds(pl.multiple_of(pair * 2 * cols, 128), 2 * cols)
        found = jnp.transpose(w_ref[:, columns])
        wt[2 * pair] = found[:cols]
        wt[2 * pair + 1] = found[cols:]
        return carry

    lax.fori_loop(0, n // 2, transpose_pair, 0)

    def region(y_of, x_of, core_of):
        return y_of * 8 + core_of * 4 + x_of

    def region_rows(number):
        return pl.ds(pl.multiple_of(number * w_rows, 16), w_rows)

    def there(number):
        return number * w_rows < cols

    mine = region(y, x, core)

    def z_copy(other):
        return remote(
            wt.at[other, region_rows(mine)],
            wc.at[me, region_rows(mine)],
            z_send.at[other],
            z_recv.at[me],
            (ctx, other),
        )

    def z_arrival(other):
        return remote(
            wt.at[other, region_rows(mine)],
            wc.at[other, region_rows(mine)],
            z_send.at[other],
            z_recv.at[other],
            (ctx, other),
        )

    @pl.when(there(mine))
    def _():
        wc[me, region_rows(mine)] = wt[me, region_rows(mine)]

        def start(step, carry):
            z_copy(lax.rem(me + step, n)).start()
            return carry

        lax.fori_loop(1, n, start, 0)

    def w_copy(number, send_sem, device):
        rows_of = region_rows(number)
        return remote(wc.at[:, rows_of], wc.at[:, rows_of], send_sem, w_recv.at[number], device)

    def x_stage():
        @pl.when(there(mine))
        def _():
            def wait(step, carry):
                z_arrival(lax.rem(me + step, n)).wait_recv()
                return carry

            lax.fori_loop(1, n, wait, 0)

            def start(step, carry):
                w_copy(mine, x_send.at[step], at(seg, lax.rem(x + step, 4), core)).start()
                return carry

            lax.fori_loop(1, 4, start, 0)

    def y_stage():
        def one(x_of, carry):
            number = region(y, x_of, core)

            @pl.when(there(number) & (x_of != x))
            def _():
                w_copy(number, x_send.at[0], sibling).wait_recv()

            if y_count > 1:

                @pl.when(there(number))
                def _():
                    def start(step, carry):
                        w_copy(number, y_send.at[x_of, step], y_at(step)).start()
                        return carry

                    lax.fori_loop(1, y_count, start, 0)

            return carry

        lax.fori_loop(0, 4, one, 0)

    def each_lane_region(core_of, do):
        def one(index, carry):
            y_of, x_of = lax.div(index, 4), lax.rem(index, 4)
            number = region(y_of, x_of, core_of)

            @pl.when(there(number))
            def _():
                do(number, y_of)

            return carry

        lax.fori_loop(0, 4 * y_count, one, 0)

    def c_stage():
        def hand_over(number, y_of):
            @pl.when(y_of != y)
            def _():
                w_copy(number, x_send.at[0], sibling).wait_recv()

            w_copy(number, c_send.at[number], sibling).start()

        each_lane_region(core, hand_over)

    def c_arrivals():
        def wait(number, y_of):
            w_copy(number, c_send.at[number], sibling).wait_recv()

        each_lane_region(1 - core, wait)

    def w_sent():
        @pl.when(there(mine))
        def _():
            def z_wait(step, carry):
                z_copy(lax.rem(me + step, n)).wait_send()
                return carry

            lax.fori_loop(1, n, z_wait, 0)

            def x_wait(step, carry):
                w_copy(mine, x_send.at[step], sibling).wait_send()
                return carry

            lax.fori_loop(1, 4, x_wait, 0)

        def y_wait(x_of, carry):
            number = region(y, x_of, core)

            @pl.when(there(number))
            def _():
                def wait(step, carry):
                    w_copy(number, y_send.at[x_of, step], sibling).wait_send()
                    return carry

                lax.fori_loop(1, y_count, wait, 0)

            return carry

        if y_count > 1:
            lax.fori_loop(0, 4, y_wait, 0)
        each_lane_region(core, lambda number, y_of: w_copy(number, c_send.at[number], sibling).wait_send())

    query_at = lax.broadcasted_iota(jnp.int32, (1, rows), 1)
    start = jnp.zeros((1, rows), jnp.int32)
    end = 0
    for doc in range(docs_ref.shape[0]):
        end = end + docs_ref[doc]
        start = jnp.where(end <= query_at + first_pos, end, start)
    start = start - first_pos
    key_at = lax.broadcasted_iota(jnp.int32, (rows, rows), 0)

    extra_row = lax.broadcasted_iota(jnp.int32, (EXTRA, rows), 0)
    extra_col = lax.broadcasted_iota(jnp.int32, (EXTRA, rows), 1)

    def key_rows(number):
        low = lax.rem(extra_col, 16)
        high = extra_col - low - (number + 1) * rows
        ones = jnp.where(extra_row < 9, 1, 0)
        picked = jnp.where(extra_row < 3, high, jnp.where(extra_row < 6, low, ones))
        return picked.astype(jnp.float32).astype(jnp.bfloat16)

    def prepare(head, carry):
        base = (me * head_count + head) * 4
        whole = slopes_ref[base]
        here = part_of(q_ref, head)[...].astype(jnp.float32) * (LOG2E / math.sqrt(HD))
        high = here.astype(jnp.bfloat16)
        low = (here - high.astype(jnp.float32)).astype(jnp.bfloat16)
        shift = -whole * extra_col.astype(jnp.float32)
        shift_1 = shift.astype(jnp.bfloat16).astype(jnp.float32)
        shift_2 = (shift - shift_1).astype(jnp.bfloat16).astype(jnp.float32)
        shift_3 = shift - shift_1 - shift_2
        which = lax.rem(extra_row, 3)
        slope = jnp.where(
            which == 0, slopes_ref[base + 1], jnp.where(which == 1, slopes_ref[base + 2], slopes_ref[base + 3])
        )
        moved = jnp.where(which == 0, shift_1, jnp.where(which == 1, shift_2, shift_3))
        rows_of = jnp.where(extra_row < 6, slope, jnp.where(extra_row < 9, moved, 0.0))
        qx[head, pl.ds(0, HD)] = high
        qx[head, pl.ds(HD, EXTRA)] = rows_of.astype(jnp.bfloat16)
        qx[head, pl.ds(HD + EXTRA, HD)] = low
        qx[head, pl.ds(2 * HD + EXTRA, EXTRA)] = jnp.zeros((EXTRA, rows), jnp.bfloat16)
        return carry

    lax.fori_loop(0, head_count, prepare, 0)

    def score(keys, number, head):
        keys = jnp.concatenate([keys, key_rows(number)], axis=0)
        keys = jnp.transpose(keys)
        keys = jnp.concatenate([keys, keys], axis=1)
        return jnp.dot(keys, qx[head], preferred_element_type=jnp.float32)

    def own_block(head, carry):
        for kv in range(2):

            @pl.when(x == 1)
            def _():
                arrived(N2, head, kv)
                copy(SECOND, slot.at[N2, kv], N4, head, kv, at(seg, 2, core)).start()

        found = score(part_of(own.at[0], head)[...], -1, head)
        allowed = (key_at <= query_at) & (key_at >= start)
        found = jnp.where(allowed, found, NEVER)
        most = jnp.max(found, axis=0, keepdims=True)
        weights = jnp.exp2(found - most)
        total[head] = jnp.sum(weights, axis=0, keepdims=True)
        top[head] = most
        part_of(acc, head)[...] = jnp.dot(
            part_of(own.at[1], head)[...], weights.astype(jnp.bfloat16), preferred_element_type=jnp.float32
        )
        return carry

    lax.fori_loop(0, head_count, own_block, 0)
    x_stage()
    y_stage()

    def bring(head, kv):
        @pl.when((ctx >= 2) & (x != 1))
        def _():
            arrived(N2, head, kv)

        @pl.when(ctx >= 2)
        def _():
            copy(SIB_N2, slot.at[N2, kv], jnp.where(core == 0, N3, N1), head, kv, sibling).start()

        @pl.when((x == 0) & has_prev)
        def _():
            copy(SECOND, slot.at[N2, kv], N4, head, kv, at(seg, 1, core)).start()

        @pl.when(ctx >= 4)
        def _():
            arrived(N4, head, kv)

        @pl.when((ctx >= 4) & (core == 1))
        def _():
            copy(SIB_N4, slot.at[N4, kv], N3, head, kv, sibling).start()

        @pl.when(ctx >= 1)
        def _():
            arrived(N1, head, kv)

        @pl.when(ctx >= 3)
        def _():
            arrived(N3, head, kv)

    def earlier_blocks(head, carry):
        bring(head, 0)
        most = top[head]
        for number in range(4):
            found = score(part_of(slot.at[number, 0], head)[...], number, head)
            found = jnp.where(key_at >= start + (number + 1) * rows, found, NEVER)
            scores[number] = found
            most = jnp.maximum(most, jnp.max(found, axis=0, keepdims=True))
        factor = jnp.exp2(top[head] - most)
        added = total[head] * factor
        for number in range(4):
            weights = jnp.exp2(scores[number] - most)
            added = added + jnp.sum(weights, axis=0, keepdims=True)
            probs[number] = weights.astype(jnp.bfloat16)
        bring(head, 1)

        @pl.when((head == head_count - 1) & gives)
        def _():
            for x_of in (2, 3):
                pl.semaphore_signal(go, inc=1, device_id=at(seg, x_of, core), device_id_type=MESH)

        @pl.when((head == head_count - 1) & gives_first)
        def _():
            for x_of in range(4):
                pl.semaphore_signal(go, inc=1, device_id=at(0, x_of, core), device_id_type=MESH)

        summed = part_of(acc, head)[...] * factor
        for number in range(4):
            summed = summed + jnp.dot(
                part_of(slot.at[number, 1], head)[...], probs[number], preferred_element_type=jnp.float32
            )
        attended = (summed / added).astype(jnp.bfloat16)
        part_of(first_half, head)[...] = attended[:, : 2 * piece_len]
        for piece in range(2):
            part_of(spread.at[me, piece], head)[...] = attended[:, (2 + piece) * piece_len : (3 + piece) * piece_len]

        return carry

    lax.fori_loop(0, head_count, earlier_blocks, 0)

    @pl.when(held)
    def _():
        pl.semaphore_wait(go, 1)

    places = ((ctx, me + 1), (ctx, me - 1))
    below = (me, n - 1 - me)

    def spread_copy(way, source, piece):
        ref = spread.at[source, piece]
        return remote(ref, ref, spread_send.at[way, source, piece], spread_recv.at[source, piece], places[way])

    def part_copy(way, owner, piece):
        return remote(
            part.at[owner, piece],
            came.at[way, owner, piece],
            part_send.at[owner, piece],
            part_recv.at[way, owner, piece],
            places[way],
        )

    for piece in range(2):
        for way in (UP, DOWN):

            @pl.when(below[way] < n - 1)
            def _():
                spread_copy(way, me, piece).start()

    c_stage()

    def partials(owner, carry):
        found = jnp.dot(wt[owner], first_half[...], preferred_element_type=jnp.float32).astype(jnp.bfloat16)
        for piece in range(2):
            part[owner, piece] = found[:, piece * piece_len : (piece + 1) * piece_len]
        return carry

    lax.fori_loop(0, n, partials, 0)
    for piece in range(2):
        second_half[piece] = jnp.dot(wt[me], spread[me, piece], preferred_element_type=jnp.float32)
    def slot_of(time, carry):
        number, piece = lax.div(time, 2), lax.rem(time, 2)
        for way in (UP, DOWN):
            behind = below[way]
            sign = 1 - 2 * way
            source = me - sign * number

            @pl.when(number <= behind)
            def _():
                spread_copy(way, source, piece).wait_recv()

            @pl.when((number <= behind) & (behind < n - 1))
            def _():
                spread_copy(way, source, piece).start()

            owner = jnp.where(way == UP, n - 1, 0) - sign * (number - behind - 1)
            sums = (number > behind) & (behind < n - 1)

            @pl.when(sums & (behind > 0))
            def _():
                part_copy(way, owner, piece).wait_recv()
                summed = part[owner, piece].astype(jnp.float32) + came[way, owner, piece].astype(jnp.float32)
                part[owner, piece] = summed.astype(jnp.bfloat16)

            @pl.when(sums)
            def _():
                part_copy(way, owner, piece).start()

        return carry

    lag = min(4, 2 * n - 2)

    def product(time, carry):
        number, piece = lax.div(time, 2), lax.rem(time, 2)
        for way in (UP, DOWN):
            source = me - (1 - 2 * way) * number

            @pl.when(number <= below[way])
            def _():
                second_half[piece] += jnp.dot(wc[source], spread[source, piece], preferred_element_type=jnp.float32)

        return carry

    lax.fori_loop(2, 2 + lag, slot_of, 0)
    c_arrivals()
    lax.fori_loop(2 + lag, 2 * n, lambda time, carry: product(time - lag, slot_of(time, carry)), 0)
    lax.fori_loop(2 * n - lag, 2 * n, product, 0)

    for piece in range(2):
        for way in (UP, DOWN):

            @pl.when(below[way] > 0)
            def _():
                part_copy(way, me, piece).wait_recv()

        whole = part[me, piece].astype(jnp.float32)
        for way in (UP, DOWN):
            whole = whole + jnp.where(below[way] > 0, came[way, me, piece].astype(jnp.float32), 0.0)
        o_ref[:, piece * piece_len : (piece + 1) * piece_len] = whole.astype(jnp.bfloat16)
        o_ref[:, (2 + piece) * piece_len : (3 + piece) * piece_len] = second_half[piece].astype(jnp.bfloat16)

    def sent(head, carry):
        for kv, ref in enumerate((k_hbm, v_hbm)):
            for what, does in (
                (OWN_A, a_does),
                (OWN_B, b_does),
                (CROSSES, crosses),
                (PASSED, passes),
                (SECOND, second),
                (SIB_OWN, core == 0),
                (SIB_N2, ctx >= 2),
                (SIB_N4, (ctx >= 4) & (core == 1)),
            ):

                @pl.when(does)
                def _():
                    copy(what, ref, N1, head, kv, sibling).wait_send()

        return carry

    lax.fori_loop(0, head_count, sent, 0)
    w_sent()

    def sums_sent(other, carry):
        for piece in range(2):

            @pl.when(other != me)
            def _():
                part_copy(UP, other, piece).wait_send()

            for way in (UP, DOWN):
                sign = 1 - 2 * way
                passed = (below[way] < n - 1) & ((me - other) * sign >= 0)

                @pl.when(passed)
                def _():
                    spread_copy(way, other, piece).wait_send()

        return carry

    lax.fori_loop(0, n, sums_sent, 0)


def layer(doc_lengths, slopes, queries, keys, values, out_weight):
    cols, rows = queries.shape
    heads = cols // HD
    n = out_weight.shape[1] // cols
    y_count = max(1, lax.axis_size("ctx") // 16)
    regions = 8 * y_count
    piece = rows // PIECES
    bf16, f32 = jnp.bfloat16, jnp.float32
    vmem, smem = pl.BlockSpec(memory_space=pltpu.VMEM), pl.BlockSpec(memory_space=pltpu.SMEM)
    anywhere = pl.BlockSpec(memory_space=pl.ANY)
    dma = pltpu.SemaphoreType.DMA
    return pl.pallas_call(
        layer_kernel,
        out_shape=jax.ShapeDtypeStruct((cols, rows), bf16),
        in_specs=[smem, smem, anywhere, anywhere, anywhere, anywhere],
        out_specs=vmem,
        scratch_shapes=[
            pltpu.VMEM((cols, rows), bf16),
            pltpu.VMEM((2, cols, rows), bf16),
            pltpu.VMEM((cols, n * cols), bf16),
            pltpu.VMEM((5, 2, cols, rows), bf16),
            pltpu.VMEM((heads, 2 * (HD + EXTRA), rows), bf16),
            pltpu.VMEM((4, rows, rows), f32),
            pltpu.VMEM((4, rows, rows), bf16),
            pltpu.VMEM((cols, rows), f32),
            pltpu.VMEM((heads, 1, rows), f32),
            pltpu.VMEM((heads, 1, rows), f32),
            pltpu.VMEM((n, cols, cols), bf16),
            pltpu.VMEM((n, cols, cols), bf16),
            pltpu.VMEM((cols, 2 * piece), bf16),
            pltpu.VMEM((n, 2, cols, piece), bf16),
            pltpu.VMEM((n, 2, cols, piece), bf16),
            pltpu.VMEM((2, n, 2, cols, piece), bf16),
            pltpu.VMEM((2, cols, piece), f32),
            dma((4,)),
            dma((8, 2, heads)),
            dma((5, 2, heads)),
            dma((n,)),
            dma((n,)),
            dma((4,)),
            dma((4, y_count)),
            dma((regions,)),
            dma((regions,)),
            dma((2, n, 2)),
            dma((n, 2)),
            dma((n, 2)),
            dma((2, n, 2)),
            pltpu.SemaphoreType.REGULAR,
        ],
        compiler_params=pltpu.CompilerParams(
            collective_id=0, has_side_effects=True, vmem_limit_bytes=56 << 20
        ),
    )(doc_lengths, slopes, queries, keys, values, out_weight)


def body(queries, keys, values, out_weight, doc_lengths):
    all_heads = queries.shape[1] // HD * lax.axis_size("tp")
    slopes = jnp.asarray(slope_table(all_heads))
    return layer(doc_lengths, slopes, queries.T, keys.T, values.T, out_weight).T


def solution(mesh):
    placed = (P("ctx", "tp"), P("ctx", "tp"), P("ctx", "tp"), P("tp", None), P())
    return jax.shard_map(
        body, mesh=mesh, in_specs=placed, out_specs=P("ctx", "tp"), check_vma=False
    )
```

```python
import functools
import math

import jax
import jax.numpy as jnp
import numpy as np
from jax import lax
from jax.experimental import pallas as pl
from jax.experimental.pallas import tpu as pltpu
from jax.sharding import PartitionSpec as P

HD = 112
EXTRA = 16
MESH = pl.DeviceIdType.MESH
LOG2E = math.log2(math.e)
NEVER = -1e30
N1, N2, N3, N4, PASS = range(5)
OWN_A, OWN_B, CROSSES, PASSED, SECOND, SIB_OWN, SIB_N2, SIB_N4 = range(8)
UP, DOWN = range(2)
PIECES = 4


def slope_table(all_heads):
    heads = np.arange(all_heads, dtype=np.float64)
    whole = (2.0 ** (-4.0 * (heads + 1.0 + all_heads) / all_heads) * LOG2E).astype(np.float32)
    rest, terms = whole.copy(), []
    for _ in range(3):
        term = rest.astype(jnp.bfloat16).astype(np.float32)
        terms.append(term)
        rest = rest - term
    return np.stack([whole, *terms], axis=1).reshape(-1)


def weight_rows(cols, y_count):
    return 16 * -(-cols // (16 * 8 * y_count))


def layer_kernel(
    docs_ref, slopes_ref, q_hbm, k_hbm, v_hbm, w_hbm, o_ref,
    q_ref, own, w_ref, slot, qx, scores, probs, acc, top, total,
    wt, wc, first_half, spread, part, came, second_half,
    load, send, recv, z_send, z_recv, x_send, y_send, c_send, w_recv, spread_send, spread_recv, part_send, part_recv,
):
    cols, rows = q_ref.shape
    head_count = cols // HD
    n = wt.shape[0]
    piece_len = rows // PIECES
    ctx, me = lax.axis_index("ctx"), lax.axis_index("tp")
    segs = lax.axis_size("ctx") // 8
    y_count = max(1, segs // 2)
    w_rows = weight_rows(cols, y_count)
    seg, x, core = lax.div(ctx, 8), lax.rem(lax.div(ctx, 2), 4), lax.rem(ctx, 2)
    y = lax.div(ctx, 16)
    has_next, has_prev = seg < segs - 1, seg > 0
    first_pos = ctx * rows

    def at(seg_of, x_of, core_of):
        return (seg_of * 8 + x_of * 2 + core_of, me)

    sibling = at(seg, x, 1 - core)
    upper = lax.rem(seg, 2) == 1
    crosses = (x >= 2) & has_next
    on_column = lax.rem(x, 2) != core
    goes_round = crosses & on_column & jnp.logical_not(upper)
    pass_x = jnp.where(x == 3, jnp.where(core == 1, 0, 3), jnp.where(core == 1, 2, 1))
    x_slot = jnp.where((x == 0) | (x == 3), N2, N4)
    c_dst = at(
        jnp.where(goes_round, seg + 1, jnp.where(upper, seg + 2, seg)), jnp.where(goes_round, 0, pass_x), core
    )
    c_slot = jnp.where(goes_round, x_slot, PASS)
    passes = on_column & (jnp.where(upper, seg, 0) != 1) & (upper | (x < 2) & has_next)
    p_source = at(jnp.where(upper, seg - 2, seg), jnp.where((x == 0) | (x == 3), 3, 2), core)
    p_dst = at(jnp.where(upper, seg - 1, seg + 1), 0, core)
    a_does = x < 3
    b_does = x == 1
    second = (x == 0) & has_prev | (x == 1)

    barrier = pltpu.get_barrier_semaphore()

    def greet(condition, device):
        @pl.when(condition)
        def _():
            pl.semaphore_signal(barrier, inc=1, device_id=device, device_id_type=MESH)

    pl.semaphore_signal(barrier, inc=1, device_id=sibling, device_id_type=MESH)
    if segs > 1:
        greet(passes, p_source)
        for x_of in (jnp.where(core == 1, 0, 3), jnp.where(core == 1, 2, 1)):
            greet((x == 0) & has_prev, at(jnp.where(upper, seg - 1, seg + 1), x_of, core))

    def greet_x(step, carry):
        pl.semaphore_signal(barrier, inc=1, device_id=at(seg, lax.rem(x + step, 4), core), device_id_type=MESH)
        return carry

    lax.fori_loop(1, 4, greet_x, 0)

    def y_at(step):
        return (lax.rem(ctx + step * 16, y_count * 16), me)

    def greet_y(step, carry):
        pl.semaphore_signal(barrier, inc=1, device_id=y_at(step), device_id_type=MESH)
        return carry

    if y_count > 1:
        lax.fori_loop(1, y_count, greet_y, 0)

    def greet_z(step, carry):
        pl.semaphore_signal(barrier, inc=1, device_id=(ctx, lax.rem(me + step, n)), device_id_type=MESH)
        return carry

    lax.fori_loop(1, n, greet_z, 0)

    loads = [
        pltpu.make_async_copy(k_hbm, own.at[0], load.at[0]),
        pltpu.make_async_copy(v_hbm, own.at[1], load.at[1]),
        pltpu.make_async_copy(q_hbm, q_ref, load.at[2]),
        pltpu.make_async_copy(w_hbm, w_ref, load.at[3]),
    ]
    for one in loads:
        one.start()

    loads[3].wait()
    def transpose_pair(pair, carry):
        columns = pl.ds(pl.multiple_of(pair * 2 * cols, 128), 2 * cols)
        found = jnp.transpose(w_ref[:, columns])
        wt[2 * pair, :, :cols] = found[:cols]
        wt[2 * pair + 1, :, :cols] = found[cols:]
        return carry

    lax.fori_loop(0, n // 2, transpose_pair, 0)
    crossing = crosses.astype(jnp.int32) + passes.astype(jnp.int32)
    awaited = 1 + 3 + (y_count - 1) + (n - 1) + crossing
    pl.semaphore_wait(barrier, awaited)

    def remote(src, dst, send_sem, recv_sem, device):
        return pltpu.make_async_remote_copy(
            src_ref=src, dst_ref=dst, send_sem=send_sem, recv_sem=recv_sem, device_id=device, device_id_type=MESH
        )

    def region(y_of, x_of, core_of):
        return y_of * 8 + core_of * 4 + x_of

    def region_rows(number):
        return pl.ds(pl.multiple_of(number * w_rows, 16), w_rows)

    def there(number):
        return number * w_rows < cols

    mine = region(y, x, core)

    def z_copy(other):
        return remote(
            wt.at[other, region_rows(mine)],
            wc.at[me, region_rows(mine)],
            z_send.at[other],
            z_recv.at[me],
            (ctx, other),
        )

    def z_arrival(other):
        return remote(
            wt.at[other, region_rows(mine)],
            wc.at[other, region_rows(mine)],
            z_send.at[other],
            z_recv.at[other],
            (ctx, other),
        )

    @pl.when(there(mine))
    def _():
        wc[me, region_rows(mine)] = wt[me, region_rows(mine)]

        def start(step, carry):
            z_copy(lax.rem(me + step, n)).start()
            return carry

        lax.fori_loop(1, n, start, 0)

    def part_of(ref, head):
        return ref.at[pl.ds(pl.multiple_of(head * HD, 16), HD)]

    def copy(what, src, number, head, kv, device):
        return remote(
            part_of(src, head),
            part_of(slot.at[number, kv], head),
            send.at[what, kv, head],
            recv.at[number, kv, head],
            device,
        )

    def arrived(number, head, kv):
        copy(SIB_OWN, slot.at[number, kv], number, head, kv, sibling).wait_recv()

    def send_sibling(head, carry):
        for kv, ref in enumerate((k_hbm, v_hbm)):

            @pl.when(core == 0)
            def _():
                copy(SIB_OWN, ref, N1, head, kv, sibling).start()

        return carry

    def send_own(head, carry):
        for kv, ref in enumerate((k_hbm, v_hbm)):

            @pl.when(a_does)
            def _():
                copy(OWN_A, ref, N2, head, kv, at(seg, x + 1, core)).start()

            @pl.when(b_does)
            def _():
                copy(OWN_B, ref, N4, head, kv, at(seg, x + 2, core)).start()

        return carry

    def send_over(head, carry):
        for kv, ref in enumerate((k_hbm, v_hbm)):

            @pl.when(crosses)
            def _():
                copy(CROSSES, ref, c_slot, head, kv, c_dst).start()

        return carry

    def pass_on(head, carry):
        for kv in range(2):

            @pl.when(passes)
            def _():
                arrived(PASS, head, kv)
                copy(PASSED, slot.at[PASS, kv], x_slot, head, kv, p_dst).start()

        return carry

    lax.fori_loop(0, head_count, send_over, 0)
    lax.fori_loop(0, head_count, send_sibling, 0)
    lax.fori_loop(0, head_count, pass_on, 0)
    for number in range(4):

        @pl.when(ctx < number + 1)
        def _():
            slot[number] = jnp.zeros(slot.shape[1:], slot.dtype)

    for one in loads[:3]:
        one.wait()

    def w_copy(number, send_sem, device):
        rows_of = region_rows(number)
        return remote(wc.at[:, rows_of], wc.at[:, rows_of], send_sem, w_recv.at[number], device)

    def x_stage():
        @pl.when(there(mine))
        def _():
            def wait(step, carry):
                z_arrival(lax.rem(me + step, n)).wait_recv()
                return carry

            lax.fori_loop(1, n, wait, 0)

            def start(step, carry):
                w_copy(mine, x_send.at[step], at(seg, lax.rem(x + step, 4), core)).start()
                return carry

            lax.fori_loop(1, 4, start, 0)

    def y_stage():
        def one(x_of, carry):
            number = region(y, x_of, core)

            @pl.when(there(number) & (x_of != x))
            def _():
                w_copy(number, x_send.at[0], sibling).wait_recv()

            if y_count > 1:

                @pl.when(there(number))
                def _():
                    def start(step, carry):
                        w_copy(number, y_send.at[x_of, step], y_at(step)).start()
                        return carry

                    lax.fori_loop(1, y_count, start, 0)

            return carry

        lax.fori_loop(0, 4, one, 0)

    def each_lane_region(core_of, do):
        def one(index, carry):
            y_of, x_of = lax.div(index, 4), lax.rem(index, 4)
            number = region(y_of, x_of, core_of)

            @pl.when(there(number))
            def _():
                do(number, y_of)

            return carry

        lax.fori_loop(0, 4 * y_count, one, 0)

    def c_stage():
        def hand_over(number, y_of):
            @pl.when(y_of != y)
            def _():
                w_copy(number, x_send.at[0], sibling).wait_recv()

            w_copy(number, c_send.at[number], sibling).start()

        each_lane_region(core, hand_over)

    def c_arrivals():
        def wait(number, y_of):
            w_copy(number, c_send.at[number], sibling).wait_recv()

        each_lane_region(1 - core, wait)

    def w_sent():
        @pl.when(there(mine))
        def _():
            def z_wait(step, carry):
                z_copy(lax.rem(me + step, n)).wait_send()
                return carry

            lax.fori_loop(1, n, z_wait, 0)

            def x_wait(step, carry):
                w_copy(mine, x_send.at[step], sibling).wait_send()
                return carry

            lax.fori_loop(1, 4, x_wait, 0)

        def y_wait(x_of, carry):
            number = region(y, x_of, core)

            @pl.when(there(number))
            def _():
                def wait(step, carry):
                    w_copy(number, y_send.at[x_of, step], sibling).wait_send()
                    return carry

                lax.fori_loop(1, y_count, wait, 0)

            return carry

        if y_count > 1:
            lax.fori_loop(0, 4, y_wait, 0)
        each_lane_region(core, lambda number, y_of: w_copy(number, c_send.at[number], sibling).wait_send())

    query_at = lax.broadcasted_iota(jnp.int32, (1, rows), 1)
    start = jnp.zeros((1, rows), jnp.int32)
    end = 0
    for doc in range(docs_ref.shape[0]):
        end = end + docs_ref[doc]
        start = jnp.where(end <= query_at + first_pos, end, start)
    start = start - first_pos
    key_at = lax.broadcasted_iota(jnp.int32, (rows, rows), 0)

    extra_row = lax.broadcasted_iota(jnp.int32, (EXTRA, rows), 0)
    extra_col = lax.broadcasted_iota(jnp.int32, (EXTRA, rows), 1)

    def key_rows(number):
        low = lax.rem(extra_col, 16)
        high = extra_col - low - (number + 1) * rows
        ones = jnp.where(extra_row < 9, 1, 0)
        picked = jnp.where(extra_row < 3, high, jnp.where(extra_row < 6, low, ones))
        return picked.astype(jnp.float32).astype(jnp.bfloat16)

    def prepare(head, carry):
        base = (me * head_count + head) * 4
        whole = slopes_ref[base]
        here = part_of(q_ref, head)[...].astype(jnp.float32) * (LOG2E / math.sqrt(HD))
        high = here.astype(jnp.bfloat16)
        low = (here - high.astype(jnp.float32)).astype(jnp.bfloat16)
        shift = -whole * extra_col.astype(jnp.float32)
        shift_1 = shift.astype(jnp.bfloat16).astype(jnp.float32)
        shift_2 = (shift - shift_1).astype(jnp.bfloat16).astype(jnp.float32)
        shift_3 = shift - shift_1 - shift_2
        which = lax.rem(extra_row, 3)
        slope = jnp.where(
            which == 0, slopes_ref[base + 1], jnp.where(which == 1, slopes_ref[base + 2], slopes_ref[base + 3])
        )
        moved = jnp.where(which == 0, shift_1, jnp.where(which == 1, shift_2, shift_3))
        rows_of = jnp.where(extra_row < 6, slope, jnp.where(extra_row < 9, moved, 0.0))
        qx[head, pl.ds(0, HD)] = high
        qx[head, pl.ds(HD, EXTRA)] = rows_of.astype(jnp.bfloat16)
        qx[head, pl.ds(HD + EXTRA, HD)] = low
        qx[head, pl.ds(2 * HD + EXTRA, EXTRA)] = jnp.zeros((EXTRA, rows), jnp.bfloat16)
        return carry

    lax.fori_loop(0, head_count, prepare, 0)

    def score(keys, number, head):
        keys = jnp.concatenate([keys, key_rows(number)], axis=0)
        keys = jnp.transpose(keys)
        keys = jnp.concatenate([keys, keys], axis=1)
        return jnp.dot(keys, qx[head], preferred_element_type=jnp.float32)

    def own_block(head, carry):
        found = score(part_of(own.at[0], head)[...], -1, head)
        allowed = (key_at <= query_at) & (key_at >= start)
        found = jnp.where(allowed, found, NEVER)
        most = jnp.max(found, axis=0, keepdims=True)
        weights = jnp.exp2(found - most)
        total[head] = jnp.sum(weights, axis=0, keepdims=True)
        top[head] = most
        part_of(acc, head)[...] = jnp.dot(
            part_of(own.at[1], head)[...], weights.astype(jnp.bfloat16), preferred_element_type=jnp.float32
        )
        return carry

    lax.fori_loop(0, head_count // 2, own_block, 0)
    x_stage()
    lax.fori_loop(0, head_count, send_own, 0)
    lax.fori_loop(head_count // 2, head_count, own_block, 0)
    y_stage()

    def hand_on(head, carry):
        for kv in range(2):
            arrived(N2, head, kv)
            copy(SECOND, slot.at[N2, kv], N4, head, kv, at(seg, 2, core)).start()
        return carry

    @pl.when(x == 1)
    def _():
        lax.fori_loop(0, head_count, hand_on, 0)

    def bring(head, kv):
        @pl.when((ctx >= 2) & (x != 1))
        def _():
            arrived(N2, head, kv)

        @pl.when(ctx >= 2)
        def _():
            copy(SIB_N2, slot.at[N2, kv], jnp.where(core == 0, N3, N1), head, kv, sibling).start()

        @pl.when((x == 0) & has_prev)
        def _():
            copy(SECOND, slot.at[N2, kv], N4, head, kv, at(seg, 1, core)).start()

        @pl.when(ctx >= 4)
        def _():
            arrived(N4, head, kv)

        @pl.when((ctx >= 4) & (core == 1))
        def _():
            copy(SIB_N4, slot.at[N4, kv], N3, head, kv, sibling).start()

        @pl.when(ctx >= 1)
        def _():
            arrived(N1, head, kv)

        @pl.when(ctx >= 3)
        def _():
            arrived(N3, head, kv)

    def earlier_blocks(head, carry):
        bring(head, 0)
        most = top[head]
        for number in range(4):
            found = score(part_of(slot.at[number, 0], head)[...], number, head)
            found = jnp.where(key_at >= start + (number + 1) * rows, found, NEVER)
            scores[number] = found
            most = jnp.maximum(most, jnp.max(found, axis=0, keepdims=True))
        factor = jnp.exp2(top[head] - most)
        added = total[head] * factor
        for number in range(4):
            weights = jnp.exp2(scores[number] - most)
            added = added + jnp.sum(weights, axis=0, keepdims=True)
            probs[number] = weights.astype(jnp.bfloat16)
        bring(head, 1)

        summed = part_of(acc, head)[...] * factor
        for number in range(4):
            summed = summed + jnp.dot(
                part_of(slot.at[number, 1], head)[...], probs[number], preferred_element_type=jnp.float32
            )
        attended = (summed / added).astype(jnp.bfloat16)
        part_of(first_half, head)[...] = attended[:, : 2 * piece_len]
        for piece in range(2):
            part_of(spread.at[me, piece], head)[...] = attended[:, (2 + piece) * piece_len : (3 + piece) * piece_len]

        return carry

    lax.fori_loop(0, head_count, earlier_blocks, 0)

    places = ((ctx, me + 1), (ctx, me - 1))
    below = (me, n - 1 - me)

    def spread_copy(way, source, piece):
        ref = spread.at[source, piece]
        return remote(ref, ref, spread_send.at[way, source, piece], spread_recv.at[source, piece], places[way])

    def part_copy(way, owner, piece):
        return remote(
            part.at[owner, piece],
            came.at[way, owner, piece],
            part_send.at[owner, piece],
            part_recv.at[way, owner, piece],
            places[way],
        )

    for piece in range(2):
        for way in (UP, DOWN):

            @pl.when(below[way] < n - 1)
            def _():
                spread_copy(way, me, piece).start()

    c_stage()

    def partials(owner, carry):
        found = jnp.dot(wt[owner, :, :cols], first_half[...], preferred_element_type=jnp.float32).astype(jnp.bfloat16)
        for piece in range(2):
            part[owner, piece] = found[:, piece * piece_len : (piece + 1) * piece_len]
        return carry

    lax.fori_loop(0, n, partials, 0)
    for piece in range(2):
        second_half[piece] = jnp.dot(wt[me, :, :cols], spread[me, piece], preferred_element_type=jnp.float32)
    def slot_of(time, carry):
        number, piece = lax.div(time, 2), lax.rem(time, 2)
        for way in (UP, DOWN):
            behind = below[way]
            sign = 1 - 2 * way
            source = me - sign * number

            @pl.when(number <= behind)
            def _():
                spread_copy(way, source, piece).wait_recv()

            @pl.when((number <= behind) & (behind < n - 1))
            def _():
                spread_copy(way, source, piece).start()

            owner = jnp.where(way == UP, n - 1, 0) - sign * (number - behind - 1)
            sums = (number > behind) & (behind < n - 1)

            @pl.when(sums & (behind > 0))
            def _():
                part_copy(way, owner, piece).wait_recv()
                summed = part[owner, piece].astype(jnp.float32) + came[way, owner, piece].astype(jnp.float32)
                part[owner, piece] = summed.astype(jnp.bfloat16)

            @pl.when(sums)
            def _():
                part_copy(way, owner, piece).start()

        return carry

    lag = min(4, 2 * n - 2)

    def product(time, carry):
        number, piece = lax.div(time, 2), lax.rem(time, 2)
        for way in (UP, DOWN):
            source = me - (1 - 2 * way) * number

            @pl.when(number <= below[way])
            def _():
                second_half[piece] += jnp.dot(
                    wc[source, :, :cols], spread[source, piece], preferred_element_type=jnp.float32
                )

        return carry

    lax.fori_loop(2, 2 + lag, slot_of, 0)
    c_arrivals()
    lax.fori_loop(2 + lag, 2 * n, lambda time, carry: product(time - lag, slot_of(time, carry)), 0)
    lax.fori_loop(2 * n - lag, 2 * n, product, 0)

    for piece in range(2):
        for way in (UP, DOWN):

            @pl.when(below[way] > 0)
            def _():
                part_copy(way, me, piece).wait_recv()

        whole = part[me, piece].astype(jnp.float32)
        for way in (UP, DOWN):
            whole = whole + jnp.where(below[way] > 0, came[way, me, piece].astype(jnp.float32), 0.0)
        o_ref[:, piece * piece_len : (piece + 1) * piece_len] = whole.astype(jnp.bfloat16)
        o_ref[:, (2 + piece) * piece_len : (3 + piece) * piece_len] = second_half[piece].astype(jnp.bfloat16)

    def sent(head, carry):
        for kv, ref in enumerate((k_hbm, v_hbm)):
            for what, does in (
                (OWN_A, a_does),
                (OWN_B, b_does),
                (CROSSES, crosses),
                (PASSED, passes),
                (SECOND, second),
                (SIB_OWN, core == 0),
                (SIB_N2, ctx >= 2),
                (SIB_N4, (ctx >= 4) & (core == 1)),
            ):

                @pl.when(does)
                def _():
                    copy(what, ref, N1, head, kv, sibling).wait_send()

        return carry

    lax.fori_loop(0, head_count, sent, 0)
    w_sent()

    def sums_sent(other, carry):
        for piece in range(2):

            @pl.when(other != me)
            def _():
                part_copy(UP, other, piece).wait_send()

            for way in (UP, DOWN):
                sign = 1 - 2 * way
                passed = (below[way] < n - 1) & ((me - other) * sign >= 0)

                @pl.when(passed)
                def _():
                    spread_copy(way, other, piece).wait_send()

        return carry

    lax.fori_loop(0, n, sums_sent, 0)


def layer(doc_lengths, slopes, queries, keys, values, out_weight):
    cols, rows = queries.shape
    heads = cols // HD
    n = out_weight.shape[1] // cols
    y_count = max(1, lax.axis_size("ctx") // 16)
    regions = 8 * y_count
    piece = rows // PIECES
    lanes = 128 * -(-cols // 128)
    bf16, f32 = jnp.bfloat16, jnp.float32
    vmem, smem = pl.BlockSpec(memory_space=pltpu.VMEM), pl.BlockSpec(memory_space=pltpu.SMEM)
    anywhere = pl.BlockSpec(memory_space=pl.ANY)
    dma = pltpu.SemaphoreType.DMA
    return pl.pallas_call(
        layer_kernel,
        out_shape=jax.ShapeDtypeStruct((cols, rows), bf16),
        in_specs=[smem, smem, anywhere, anywhere, anywhere, anywhere],
        out_specs=vmem,
        scratch_shapes=[
            pltpu.VMEM((cols, rows), bf16),
            pltpu.VMEM((2, cols, rows), bf16),
            pltpu.VMEM((cols, n * cols), bf16),
            pltpu.VMEM((5, 2, cols, rows), bf16),
            pltpu.VMEM((heads, 2 * (HD + EXTRA), rows), bf16),
            pltpu.VMEM((4, rows, rows), f32),
            pltpu.VMEM((4, rows, rows), bf16),
            pltpu.VMEM((cols, rows), f32),
            pltpu.VMEM((heads, 1, rows), f32),
            pltpu.VMEM((heads, 1, rows), f32),
            pltpu.VMEM((n, cols, lanes), bf16),
            pltpu.VMEM((n, cols, lanes), bf16),
            pltpu.VMEM((cols, 2 * piece), bf16),
            pltpu.VMEM((n, 2, cols, piece), bf16),
            pltpu.VMEM((n, 2, cols, piece), bf16),
            pltpu.VMEM((2, n, 2, cols, piece), bf16),
            pltpu.VMEM((2, cols, piece), f32),
            dma((4,)),
            dma((8, 2, heads)),
            dma((5, 2, heads)),
            dma((n,)),
            dma((n,)),
            dma((4,)),
            dma((4, y_count)),
            dma((regions,)),
            dma((regions,)),
            dma((2, n, 2)),
            dma((n, 2)),
            dma((n, 2)),
            dma((2, n, 2)),
        ],
        compiler_params=pltpu.CompilerParams(
            collective_id=0, has_side_effects=True, vmem_limit_bytes=56 << 20
        ),
    )(doc_lengths, slopes, queries, keys, values, out_weight)


def body(queries, keys, values, out_weight, doc_lengths):
    all_heads = queries.shape[1] // HD * lax.axis_size("tp")
    slopes = jnp.asarray(slope_table(all_heads))
    return layer(doc_lengths, slopes, queries.T, keys.T, values.T, out_weight).T


def solution(mesh):
    placed = (P("ctx", "tp"), P("ctx", "tp"), P("ctx", "tp"), P("tp", None), P())
    return jax.shard_map(
        body, mesh=mesh, in_specs=placed, out_specs=P("ctx", "tp"), check_vma=False
    )
```

```python
import functools
import math

import jax
import jax.numpy as jnp
import numpy as np
from jax import lax
from jax.experimental import pallas as pl
from jax.experimental.pallas import tpu as pltpu
from jax.sharding import PartitionSpec as P

HD = 112
EXTRA = 16
MESH = pl.DeviceIdType.MESH
LOG2E = math.log2(math.e)
NEVER = -1e30
N1, N2, N3, N4, PASS = range(5)
OWN_A, OWN_B, CROSSES, PASSED, SECOND, SIB_OWN, SIB_N2, SIB_N4 = range(8)
UP, DOWN = range(2)
PIECES = 4


def slope_table(all_heads):
    heads = np.arange(all_heads, dtype=np.float64)
    whole = (2.0 ** (-4.0 * (heads + 1.0 + all_heads) / all_heads) * LOG2E).astype(np.float32)
    rest, terms = whole.copy(), []
    for _ in range(3):
        term = rest.astype(jnp.bfloat16).astype(np.float32)
        terms.append(term)
        rest = rest - term
    return np.stack([whole, *terms], axis=1).reshape(-1)


def weight_rows(cols, y_count):
    return 16 * -(-cols // (16 * 8 * y_count))


def layer_kernel(
    docs_ref, slopes_ref, q_hbm, k_hbm, v_hbm, w_hbm, o_ref,
    q_ref, own, w_ref, slot, qx, scores, probs, acc, top, total,
    wt, wc, first_half, spread, part, came, second_half,
    load, send, recv, z_send, z_recv, x_send, y_send, c_send, w_recv, spread_send, spread_recv, part_send, part_recv,
):
    cols, rows = q_ref.shape
    head_count = cols // HD
    n = wt.shape[0]
    piece_len = rows // PIECES
    ctx, me = lax.axis_index("ctx"), lax.axis_index("tp")
    segs = lax.axis_size("ctx") // 8
    y_count = max(1, segs // 2)
    w_rows = weight_rows(cols, y_count)
    seg, x, core = lax.div(ctx, 8), lax.rem(lax.div(ctx, 2), 4), lax.rem(ctx, 2)
    y = lax.div(ctx, 16)
    has_next, has_prev = seg < segs - 1, seg > 0
    first_pos = ctx * rows

    def at(seg_of, x_of, core_of):
        return (seg_of * 8 + x_of * 2 + core_of, me)

    sibling = at(seg, x, 1 - core)
    upper = lax.rem(seg, 2) == 1
    crosses = (x >= 2) & has_next
    on_column = lax.rem(x, 2) != core
    goes_round = crosses & on_column & jnp.logical_not(upper)
    pass_x = jnp.where(x == 3, jnp.where(core == 1, 0, 3), jnp.where(core == 1, 2, 1))
    x_slot = jnp.where((x == 0) | (x == 3), N2, N4)
    c_dst = at(
        jnp.where(goes_round, seg + 1, jnp.where(upper, seg + 2, seg)), jnp.where(goes_round, 0, pass_x), core
    )
    c_slot = jnp.where(goes_round, x_slot, PASS)
    passes = on_column & (jnp.where(upper, seg, 0) != 1) & (upper | (x < 2) & has_next)
    p_source = at(jnp.where(upper, seg - 2, seg), jnp.where((x == 0) | (x == 3), 3, 2), core)
    p_dst = at(jnp.where(upper, seg - 1, seg + 1), 0, core)
    a_does = x < 3
    b_does = x == 1
    second = (x == 0) & has_prev | (x == 1)

    barrier = pltpu.get_barrier_semaphore()

    def greet(condition, device):
        @pl.when(condition)
        def _():
            pl.semaphore_signal(barrier, inc=1, device_id=device, device_id_type=MESH)

    pl.semaphore_signal(barrier, inc=1, device_id=sibling, device_id_type=MESH)
    if segs > 1:
        greet(passes, p_source)
        for x_of in (jnp.where(core == 1, 0, 3), jnp.where(core == 1, 2, 1)):
            greet((x == 0) & has_prev, at(jnp.where(upper, seg - 1, seg + 1), x_of, core))

    def greet_x(step, carry):
        pl.semaphore_signal(barrier, inc=1, device_id=at(seg, lax.rem(x + step, 4), core), device_id_type=MESH)
        return carry

    lax.fori_loop(1, 4, greet_x, 0)

    def y_at(step):
        return (lax.rem(ctx + step * 16, y_count * 16), me)

    def greet_y(step, carry):
        pl.semaphore_signal(barrier, inc=1, device_id=y_at(step), device_id_type=MESH)
        return carry

    if y_count > 1:
        lax.fori_loop(1, y_count, greet_y, 0)

    def greet_z(step, carry):
        pl.semaphore_signal(barrier, inc=1, device_id=(ctx, lax.rem(me + step, n)), device_id_type=MESH)
        return carry

    lax.fori_loop(1, n, greet_z, 0)

    loads = [
        pltpu.make_async_copy(k_hbm, own.at[0], load.at[0]),
        pltpu.make_async_copy(v_hbm, own.at[1], load.at[1]),
        pltpu.make_async_copy(q_hbm, q_ref, load.at[2]),
        pltpu.make_async_copy(w_hbm, w_ref, load.at[3]),
    ]
    for one in loads:
        one.start()

    loads[3].wait()
    def transpose_pair(pair, carry):
        columns = pl.ds(pl.multiple_of(pair * 2 * cols, 128), 2 * cols)
        found = jnp.transpose(w_ref[:, columns])
        wt[2 * pair, :, :cols] = found[:cols]
        wt[2 * pair + 1, :, :cols] = found[cols:]
        return carry

    lax.fori_loop(0, n // 2, transpose_pair, 0)
    crossing = crosses.astype(jnp.int32) + passes.astype(jnp.int32)
    awaited = 1 + 3 + (y_count - 1) + (n - 1) + crossing
    pl.semaphore_wait(barrier, awaited)

    def remote(src, dst, send_sem, recv_sem, device):
        return pltpu.make_async_remote_copy(
            src_ref=src, dst_ref=dst, send_sem=send_sem, recv_sem=recv_sem, device_id=device, device_id_type=MESH
        )

    def region(y_of, x_of, core_of):
        return y_of * 8 + core_of * 4 + x_of

    def region_rows(number):
        return pl.ds(pl.multiple_of(number * w_rows, 16), w_rows)

    def there(number):
        return number * w_rows < cols

    mine = region(y, x, core)

    def z_copy(other):
        return remote(
            wt.at[other, region_rows(mine)],
            wc.at[me, region_rows(mine)],
            z_send.at[other],
            z_recv.at[me],
            (ctx, other),
        )

    def z_arrival(other):
        return remote(
            wt.at[other, region_rows(mine)],
            wc.at[other, region_rows(mine)],
            z_send.at[other],
            z_recv.at[other],
            (ctx, other),
        )

    @pl.when(there(mine))
    def _():
        wc[me, region_rows(mine)] = wt[me, region_rows(mine)]

        def start(step, carry):
            z_copy(lax.rem(me + step, n)).start()
            return carry

        lax.fori_loop(1, n, start, 0)

    def part_of(ref, head):
        return ref.at[pl.ds(pl.multiple_of(head * HD, 16), HD)]

    def copy(what, src, number, head, kv, device):
        return remote(
            part_of(src, head),
            part_of(slot.at[number, kv], head),
            send.at[what, kv, head],
            recv.at[number, kv, head],
            device,
        )

    def arrived(number, head, kv):
        copy(SIB_OWN, slot.at[number, kv], number, head, kv, sibling).wait_recv()

    def send_sibling(head, carry):
        for kv, ref in enumerate((k_hbm, v_hbm)):

            @pl.when(core == 0)
            def _():
                copy(SIB_OWN, ref, N1, head, kv, sibling).start()

        return carry

    def send_own(head, carry):
        for kv, ref in enumerate((k_hbm, v_hbm)):

            @pl.when(a_does)
            def _():
                copy(OWN_A, ref, N2, head, kv, at(seg, x + 1, core)).start()

            @pl.when(b_does)
            def _():
                copy(OWN_B, ref, N4, head, kv, at(seg, x + 2, core)).start()

        return carry

    def send_over(head, carry):
        for kv, ref in enumerate((k_hbm, v_hbm)):

            @pl.when(crosses)
            def _():
                copy(CROSSES, ref, c_slot, head, kv, c_dst).start()

        return carry

    def pass_on(head, carry):
        for kv in range(2):

            @pl.when(passes)
            def _():
                arrived(PASS, head, kv)
                copy(PASSED, slot.at[PASS, kv], x_slot, head, kv, p_dst).start()

        return carry

    lax.fori_loop(0, head_count, send_over, 0)
    lax.fori_loop(0, head_count, send_sibling, 0)
    lax.fori_loop(0, head_count, pass_on, 0)
    for number in range(4):

        @pl.when(ctx < number + 1)
        def _():
            slot[number] = jnp.zeros(slot.shape[1:], slot.dtype)

    for one in loads[:3]:
        one.wait()

    def w_copy(number, send_sem, device):
        rows_of = region_rows(number)
        return remote(wc.at[:, rows_of], wc.at[:, rows_of], send_sem, w_recv.at[number], device)

    def x_stage():
        @pl.when(there(mine))
        def _():
            def wait(step, carry):
                z_arrival(lax.rem(me + step, n)).wait_recv()
                return carry

            lax.fori_loop(1, n, wait, 0)

            def start(step, carry):
                w_copy(mine, x_send.at[step], at(seg, lax.rem(x + step, 4), core)).start()
                return carry

            lax.fori_loop(1, 4, start, 0)

    def y_stage():
        def one(x_of, carry):
            number = region(y, x_of, core)

            @pl.when(there(number) & (x_of != x))
            def _():
                w_copy(number, x_send.at[0], sibling).wait_recv()

            if y_count > 1:

                @pl.when(there(number))
                def _():
                    def start(step, carry):
                        w_copy(number, y_send.at[x_of, step], y_at(step)).start()
                        return carry

                    lax.fori_loop(1, y_count, start, 0)

            return carry

        lax.fori_loop(0, 4, one, 0)

    def each_lane_region(core_of, do):
        def one(index, carry):
            y_of, x_of = lax.div(index, 4), lax.rem(index, 4)
            number = region(y_of, x_of, core_of)

            @pl.when(there(number))
            def _():
                do(number, y_of)

            return carry

        lax.fori_loop(0, 4 * y_count, one, 0)

    def c_stage():
        def hand_over(number, y_of):
            @pl.when(y_of != y)
            def _():
                w_copy(number, x_send.at[0], sibling).wait_recv()

            w_copy(number, c_send.at[number], sibling).start()

        each_lane_region(core, hand_over)

    def c_arrivals():
        def wait(number, y_of):
            w_copy(number, c_send.at[number], sibling).wait_recv()

        each_lane_region(1 - core, wait)

    def w_sent():
        @pl.when(there(mine))
        def _():
            def z_wait(step, carry):
                z_copy(lax.rem(me + step, n)).wait_send()
                return carry

            lax.fori_loop(1, n, z_wait, 0)

            def x_wait(step, carry):
                w_copy(mine, x_send.at[step], sibling).wait_send()
                return carry

            lax.fori_loop(1, 4, x_wait, 0)

        def y_wait(x_of, carry):
            number = region(y, x_of, core)

            @pl.when(there(number))
            def _():
                def wait(step, carry):
                    w_copy(number, y_send.at[x_of, step], sibling).wait_send()
                    return carry

                lax.fori_loop(1, y_count, wait, 0)

            return carry

        if y_count > 1:
            lax.fori_loop(0, 4, y_wait, 0)
        each_lane_region(core, lambda number, y_of: w_copy(number, c_send.at[number], sibling).wait_send())

    query_at = lax.broadcasted_iota(jnp.int32, (1, rows), 1)
    start = jnp.zeros((1, rows), jnp.int32)
    end = 0
    for doc in range(docs_ref.shape[0]):
        end = end + docs_ref[doc]
        start = jnp.where(end <= query_at + first_pos, end, start)
    start = start - first_pos
    key_at = lax.broadcasted_iota(jnp.int32, (rows, rows), 0)

    extra_row = lax.broadcasted_iota(jnp.int32, (EXTRA, rows), 0)
    extra_col = lax.broadcasted_iota(jnp.int32, (EXTRA, rows), 1)

    def key_rows(number):
        low = lax.rem(extra_col, 16)
        high = extra_col - low - (number + 1) * rows
        ones = jnp.where(extra_row < 9, 1, 0)
        picked = jnp.where(extra_row < 3, high, jnp.where(extra_row < 6, low, ones))
        return picked.astype(jnp.float32).astype(jnp.bfloat16)

    def prepare(head, carry):
        base = (me * head_count + head) * 4
        whole = slopes_ref[base]
        here = part_of(q_ref, head)[...].astype(jnp.float32) * (LOG2E / math.sqrt(HD))
        high = here.astype(jnp.bfloat16)
        low = (here - high.astype(jnp.float32)).astype(jnp.bfloat16)
        shift = -whole * extra_col.astype(jnp.float32)
        shift_1 = shift.astype(jnp.bfloat16).astype(jnp.float32)
        shift_2 = (shift - shift_1).astype(jnp.bfloat16).astype(jnp.float32)
        shift_3 = shift - shift_1 - shift_2
        which = lax.rem(extra_row, 3)
        slope = jnp.where(
            which == 0, slopes_ref[base + 1], jnp.where(which == 1, slopes_ref[base + 2], slopes_ref[base + 3])
        )
        moved = jnp.where(which == 0, shift_1, jnp.where(which == 1, shift_2, shift_3))
        rows_of = jnp.where(extra_row < 6, slope, jnp.where(extra_row < 9, moved, 0.0))
        qx[head, pl.ds(0, HD)] = high
        qx[head, pl.ds(HD, EXTRA)] = rows_of.astype(jnp.bfloat16)
        qx[head, pl.ds(HD + EXTRA, HD)] = low
        qx[head, pl.ds(2 * HD + EXTRA, EXTRA)] = jnp.zeros((EXTRA, rows), jnp.bfloat16)
        return carry

    lax.fori_loop(0, head_count, prepare, 0)

    def score(keys, number, head):
        keys = jnp.concatenate([keys, key_rows(number)], axis=0)
        keys = jnp.transpose(keys)
        keys = jnp.concatenate([keys, keys], axis=1)
        return jnp.dot(keys, qx[head], preferred_element_type=jnp.float32)

    def own_block(head, carry):
        found = score(part_of(own.at[0], head)[...], -1, head)
        allowed = (key_at <= query_at) & (key_at >= start)
        found = jnp.where(allowed, found, NEVER)
        most = jnp.max(found, axis=0, keepdims=True)
        weights = jnp.exp2(found - most)
        total[head] = jnp.sum(weights, axis=0, keepdims=True)
        top[head] = most
        part_of(acc, head)[...] = jnp.dot(
            part_of(own.at[1], head)[...], weights.astype(jnp.bfloat16), preferred_element_type=jnp.float32
        )
        return carry

    lax.fori_loop(0, head_count, send_own, 0)
    x_stage()
    lax.fori_loop(0, head_count // 2, own_block, 0)
    lax.fori_loop(head_count // 2, head_count, own_block, 0)

    def hand_on(head, carry):
        for kv in range(2):
            arrived(N2, head, kv)
            copy(SECOND, slot.at[N2, kv], N4, head, kv, at(seg, 2, core)).start()
        return carry

    @pl.when(x == 1)
    def _():
        lax.fori_loop(0, head_count, hand_on, 0)

    def hand_out(head, kv):
        @pl.when((ctx >= 2) & (x != 1))
        def _():
            arrived(N2, head, kv)

        @pl.when((x == 0) & has_prev)
        def _():
            copy(SECOND, slot.at[N2, kv], N4, head, kv, at(seg, 1, core)).start()

        @pl.when(ctx >= 2)
        def _():
            copy(SIB_N2, slot.at[N2, kv], jnp.where(core == 0, N3, N1), head, kv, sibling).start()

    def bring(head, kv):
        @pl.when(ctx >= 4)
        def _():
            arrived(N4, head, kv)

        @pl.when((ctx >= 4) & (core == 1))
        def _():
            copy(SIB_N4, slot.at[N4, kv], N3, head, kv, sibling).start()

        @pl.when(ctx >= 1)
        def _():
            arrived(N1, head, kv)

        @pl.when(ctx >= 3)
        def _():
            arrived(N3, head, kv)

    def earlier_blocks(head, carry):
        hand_out(head, 0)
        hand_out(head, 1)
        bring(head, 0)
        most = top[head]
        for number in range(4):
            found = score(part_of(slot.at[number, 0], head)[...], number, head)
            found = jnp.where(key_at >= start + (number + 1) * rows, found, NEVER)
            scores[number] = found
            most = jnp.maximum(most, jnp.max(found, axis=0, keepdims=True))
        factor = jnp.exp2(top[head] - most)
        added = total[head] * factor
        for number in range(4):
            weights = jnp.exp2(scores[number] - most)
            added = added + jnp.sum(weights, axis=0, keepdims=True)
            probs[number] = weights.astype(jnp.bfloat16)
        bring(head, 1)

        summed = part_of(acc, head)[...] * factor
        for number in range(4):
            summed = summed + jnp.dot(
                part_of(slot.at[number, 1], head)[...], probs[number], preferred_element_type=jnp.float32
            )
        attended = (summed / added).astype(jnp.bfloat16)
        part_of(first_half, head)[...] = attended[:, : 2 * piece_len]
        for piece in range(2):
            part_of(spread.at[me, piece], head)[...] = attended[:, (2 + piece) * piece_len : (3 + piece) * piece_len]

        return carry

    lax.fori_loop(0, head_count, earlier_blocks, 0)

    places = ((ctx, me + 1), (ctx, me - 1))
    below = (me, n - 1 - me)

    def spread_copy(way, source, piece):
        ref = spread.at[source, piece]
        return remote(ref, ref, spread_send.at[way, source, piece], spread_recv.at[source, piece], places[way])

    def part_copy(way, owner, piece):
        return remote(
            part.at[owner, piece],
            came.at[way, owner, piece],
            part_send.at[owner, piece],
            part_recv.at[way, owner, piece],
            places[way],
        )

    for piece in range(2):
        for way in (UP, DOWN):

            @pl.when(below[way] < n - 1)
            def _():
                spread_copy(way, me, piece).start()

    y_stage()

    def partials(owner, carry):
        found = jnp.dot(wt[owner, :, :cols], first_half[...], preferred_element_type=jnp.float32).astype(jnp.bfloat16)
        for piece in range(2):
            part[owner, piece] = found[:, piece * piece_len : (piece + 1) * piece_len]
        return carry

    lax.fori_loop(0, n, partials, 0)
    for piece in range(2):
        second_half[piece] = jnp.dot(wt[me, :, :cols], spread[me, piece], preferred_element_type=jnp.float32)
    def slot_of(time, carry):
        number, piece = lax.div(time, 2), lax.rem(time, 2)
        for way in (UP, DOWN):
            behind = below[way]
            sign = 1 - 2 * way
            source = me - sign * number

            @pl.when(number <= behind)
            def _():
                spread_copy(way, source, piece).wait_recv()

            @pl.when((number <= behind) & (behind < n - 1))
            def _():
                spread_copy(way, source, piece).start()

            owner = jnp.where(way == UP, n - 1, 0) - sign * (number - behind - 1)
            sums = (number > behind) & (behind < n - 1)

            @pl.when(sums & (behind > 0))
            def _():
                part_copy(way, owner, piece).wait_recv()
                summed = part[owner, piece].astype(jnp.float32) + came[way, owner, piece].astype(jnp.float32)
                part[owner, piece] = summed.astype(jnp.bfloat16)

            @pl.when(sums)
            def _():
                part_copy(way, owner, piece).start()

        return carry

    lag = min(4, 2 * n - 2)

    def product(time, carry):
        number, piece = lax.div(time, 2), lax.rem(time, 2)
        for way in (UP, DOWN):
            source = me - (1 - 2 * way) * number

            @pl.when(number <= below[way])
            def _():
                second_half[piece] += jnp.dot(
                    wc[source, :, :cols], spread[source, piece], preferred_element_type=jnp.float32
                )

        return carry

    late = max(2, 2 * n - 4)
    lax.fori_loop(2, late, slot_of, 0)
    c_stage()
    lax.fori_loop(late, 2 * n, slot_of, 0)
    c_arrivals()
    lax.fori_loop(2, 2 * n, product, 0)
    for piece in range(2):
        for way in (UP, DOWN):

            @pl.when(below[way] > 0)
            def _():
                part_copy(way, me, piece).wait_recv()

        whole = part[me, piece].astype(jnp.float32)
        for way in (UP, DOWN):
            whole = whole + jnp.where(below[way] > 0, came[way, me, piece].astype(jnp.float32), 0.0)
        o_ref[:, piece * piece_len : (piece + 1) * piece_len] = whole.astype(jnp.bfloat16)
        o_ref[:, (2 + piece) * piece_len : (3 + piece) * piece_len] = second_half[piece].astype(jnp.bfloat16)

    def sent(head, carry):
        for kv, ref in enumerate((k_hbm, v_hbm)):
            for what, does in (
                (OWN_A, a_does),
                (OWN_B, b_does),
                (CROSSES, crosses),
                (PASSED, passes),
                (SECOND, second),
                (SIB_OWN, core == 0),
                (SIB_N2, ctx >= 2),
                (SIB_N4, (ctx >= 4) & (core == 1)),
            ):

                @pl.when(does)
                def _():
                    copy(what, ref, N1, head, kv, sibling).wait_send()

        return carry

    lax.fori_loop(0, head_count, sent, 0)
    w_sent()

    def sums_sent(other, carry):
        for piece in range(2):

            @pl.when(other != me)
            def _():
                part_copy(UP, other, piece).wait_send()

            for way in (UP, DOWN):
                sign = 1 - 2 * way
                passed = (below[way] < n - 1) & ((me - other) * sign >= 0)

                @pl.when(passed)
                def _():
                    spread_copy(way, other, piece).wait_send()

        return carry

    lax.fori_loop(0, n, sums_sent, 0)


def layer(doc_lengths, slopes, queries, keys, values, out_weight):
    cols, rows = queries.shape
    heads = cols // HD
    n = out_weight.shape[1] // cols
    y_count = max(1, lax.axis_size("ctx") // 16)
    regions = 8 * y_count
    piece = rows // PIECES
    lanes = 128 * -(-cols // 128)
    bf16, f32 = jnp.bfloat16, jnp.float32
    vmem, smem = pl.BlockSpec(memory_space=pltpu.VMEM), pl.BlockSpec(memory_space=pltpu.SMEM)
    anywhere = pl.BlockSpec(memory_space=pl.ANY)
    dma = pltpu.SemaphoreType.DMA
    return pl.pallas_call(
        layer_kernel,
        out_shape=jax.ShapeDtypeStruct((cols, rows), bf16),
        in_specs=[smem, smem, anywhere, anywhere, anywhere, anywhere],
        out_specs=vmem,
        scratch_shapes=[
            pltpu.VMEM((cols, rows), bf16),
            pltpu.VMEM((2, cols, rows), bf16),
            pltpu.VMEM((cols, n * cols), bf16),
            pltpu.VMEM((5, 2, cols, rows), bf16),
            pltpu.VMEM((heads, 2 * (HD + EXTRA), rows), bf16),
            pltpu.VMEM((4, rows, rows), f32),
            pltpu.VMEM((4, rows, rows), bf16),
            pltpu.VMEM((cols, rows), f32),
            pltpu.VMEM((heads, 1, rows), f32),
            pltpu.VMEM((heads, 1, rows), f32),
            pltpu.VMEM((n, cols, lanes), bf16),
            pltpu.VMEM((n, cols, lanes), bf16),
            pltpu.VMEM((cols, 2 * piece), bf16),
            pltpu.VMEM((n, 2, cols, piece), bf16),
            pltpu.VMEM((n, 2, cols, piece), bf16),
            pltpu.VMEM((2, n, 2, cols, piece), bf16),
            pltpu.VMEM((2, cols, piece), f32),
            dma((4,)),
            dma((8, 2, heads)),
            dma((5, 2, heads)),
            dma((n,)),
            dma((n,)),
            dma((4,)),
            dma((4, y_count)),
            dma((regions,)),
            dma((regions,)),
            dma((2, n, 2)),
            dma((n, 2)),
            dma((n, 2)),
            dma((2, n, 2)),
        ],
        compiler_params=pltpu.CompilerParams(
            collective_id=0, has_side_effects=True, vmem_limit_bytes=56 << 20
        ),
    )(doc_lengths, slopes, queries, keys, values, out_weight)


def body(queries, keys, values, out_weight, doc_lengths):
    all_heads = queries.shape[1] // HD * lax.axis_size("tp")
    slopes = jnp.asarray(slope_table(all_heads))
    return layer(doc_lengths, slopes, queries.T, keys.T, values.T, out_weight).T


def solution(mesh):
    placed = (P("ctx", "tp"), P("ctx", "tp"), P("ctx", "tp"), P("tp", None), P())
    return jax.shard_map(
        body, mesh=mesh, in_specs=placed, out_specs=P("ctx", "tp"), check_vma=False
    )
```

```python
import functools
import math

import jax
import jax.numpy as jnp
import numpy as np
from jax import lax
from jax.experimental import pallas as pl
from jax.experimental.pallas import tpu as pltpu
from jax.sharding import PartitionSpec as P

HD = 112
EXTRA = 16
MESH = pl.DeviceIdType.MESH
LOG2E = math.log2(math.e)
NEVER = -1e30
N1, N2, N3, N4, PASS = range(5)
OWN_A, OWN_B, CROSSES, PASSED, SECOND, SIB_OWN, SIB_N2, SIB_N4 = range(8)
UP, DOWN = range(2)
PIECES = 4


def slope_table(all_heads):
    heads = np.arange(all_heads, dtype=np.float64)
    whole = (2.0 ** (-4.0 * (heads + 1.0 + all_heads) / all_heads) * LOG2E).astype(np.float32)
    rest, terms = whole.copy(), []
    for _ in range(3):
        term = rest.astype(jnp.bfloat16).astype(np.float32)
        terms.append(term)
        rest = rest - term
    return np.stack([whole, *terms], axis=1).reshape(-1)


def weight_rows(cols, y_count):
    return 16 * -(-cols // (16 * 8 * y_count))


def layer_kernel(
    docs_ref, slopes_ref, q_hbm, k_hbm, v_hbm, w_hbm, o_ref,
    q_ref, own, w_ref, slot, qx, scores, probs, acc, top, total,
    wt, wc, first_half, spread, part, came, second_half,
    load, send, recv, z_send, z_recv, x_send, y_send, c_send, w_recv, spread_send, spread_recv, part_send, part_recv,
):
    cols, rows = q_ref.shape
    head_count = cols // HD
    n = wt.shape[0]
    piece_len = rows // PIECES
    ctx, me = lax.axis_index("ctx"), lax.axis_index("tp")
    segs = lax.axis_size("ctx") // 8
    y_count = max(1, segs // 2)
    w_rows = weight_rows(cols, y_count)
    seg, x, core = lax.div(ctx, 8), lax.rem(lax.div(ctx, 2), 4), lax.rem(ctx, 2)
    y = lax.div(ctx, 16)
    has_next, has_prev = seg < segs - 1, seg > 0
    first_pos = ctx * rows

    def at(seg_of, x_of, core_of):
        return (seg_of * 8 + x_of * 2 + core_of, me)

    sibling = at(seg, x, 1 - core)
    upper = lax.rem(seg, 2) == 1
    crosses = (x >= 2) & has_next
    on_column = lax.rem(x, 2) != core
    goes_round = crosses & on_column & jnp.logical_not(upper)
    pass_x = jnp.where(x == 3, jnp.where(core == 1, 0, 3), jnp.where(core == 1, 2, 1))
    x_slot = jnp.where((x == 0) | (x == 3), N2, N4)
    c_dst = at(
        jnp.where(goes_round, seg + 1, jnp.where(upper, seg + 2, seg)), jnp.where(goes_round, 0, pass_x), core
    )
    c_slot = jnp.where(goes_round, x_slot, PASS)
    passes = on_column & (jnp.where(upper, seg, 0) != 1) & (upper | (x < 2) & has_next)
    p_source = at(jnp.where(upper, seg - 2, seg), jnp.where((x == 0) | (x == 3), 3, 2), core)
    p_dst = at(jnp.where(upper, seg - 1, seg + 1), 0, core)
    a_does = x < 3
    b_does = x == 1
    second = (x == 0) & has_prev | (x == 1)

    barrier = pltpu.get_barrier_semaphore()

    def greet(condition, device):
        @pl.when(condition)
        def _():
            pl.semaphore_signal(barrier, inc=1, device_id=device, device_id_type=MESH)

    pl.semaphore_signal(barrier, inc=1, device_id=sibling, device_id_type=MESH)
    if segs > 1:
        greet(passes, p_source)
        for x_of in (jnp.where(core == 1, 0, 3), jnp.where(core == 1, 2, 1)):
            greet((x == 0) & has_prev, at(jnp.where(upper, seg - 1, seg + 1), x_of, core))

    def greet_x(step, carry):
        pl.semaphore_signal(barrier, inc=1, device_id=at(seg, lax.rem(x + step, 4), core), device_id_type=MESH)
        return carry

    lax.fori_loop(1, 4, greet_x, 0)

    def y_at(step):
        return (lax.rem(ctx + step * 16, y_count * 16), me)

    def greet_y(step, carry):
        pl.semaphore_signal(barrier, inc=1, device_id=y_at(step), device_id_type=MESH)
        return carry

    if y_count > 1:
        lax.fori_loop(1, y_count, greet_y, 0)

    def greet_z(step, carry):
        pl.semaphore_signal(barrier, inc=1, device_id=(ctx, lax.rem(me + step, n)), device_id_type=MESH)
        return carry

    lax.fori_loop(1, n, greet_z, 0)

    loads = [
        pltpu.make_async_copy(k_hbm, own.at[0], load.at[0]),
        pltpu.make_async_copy(v_hbm, own.at[1], load.at[1]),
        pltpu.make_async_copy(q_hbm, q_ref, load.at[2]),
        pltpu.make_async_copy(w_hbm, w_ref, load.at[3]),
    ]
    for one in loads:
        one.start()

    def transpose_pair(pair, carry):
        columns = pl.ds(pl.multiple_of(pair * 2 * cols, 128), 2 * cols)
        found = jnp.transpose(w_ref[:, columns])
        wt[2 * pair, :, :cols] = found[:cols]
        wt[2 * pair + 1, :, :cols] = found[cols:]
        return carry

    crossing = crosses.astype(jnp.int32) + passes.astype(jnp.int32)
    awaited = 1 + 3 + (y_count - 1) + (n - 1) + crossing
    pl.semaphore_wait(barrier, awaited)

    def remote(src, dst, send_sem, recv_sem, device):
        return pltpu.make_async_remote_copy(
            src_ref=src, dst_ref=dst, send_sem=send_sem, recv_sem=recv_sem, device_id=device, device_id_type=MESH
        )

    def region(y_of, x_of, core_of):
        return y_of * 8 + core_of * 4 + x_of

    def region_rows(number):
        return pl.ds(pl.multiple_of(number * w_rows, 16), w_rows)

    def there(number):
        return number * w_rows < cols

    mine = region(y, x, core)

    def z_copy(other):
        return remote(
            wt.at[other, region_rows(mine)],
            wc.at[me, region_rows(mine)],
            z_send.at[other],
            z_recv.at[me],
            (ctx, other),
        )

    def z_arrival(other):
        return remote(
            wt.at[other, region_rows(mine)],
            wc.at[other, region_rows(mine)],
            z_send.at[other],
            z_recv.at[other],
            (ctx, other),
        )

    def part_of(ref, head):
        return ref.at[pl.ds(pl.multiple_of(head * HD, 16), HD)]

    def copy(what, src, number, head, kv, device):
        return remote(
            part_of(src, head),
            part_of(slot.at[number, kv], head),
            send.at[what, kv, head],
            recv.at[number, kv, head],
            device,
        )

    def arrived(number, head, kv):
        copy(SIB_OWN, slot.at[number, kv], number, head, kv, sibling).wait_recv()

    def send_sibling(head, carry):
        for kv, ref in enumerate((k_hbm, v_hbm)):

            @pl.when(core == 0)
            def _():
                copy(SIB_OWN, ref, N1, head, kv, sibling).start()

        return carry

    def send_own(head, carry):
        for kv, ref in enumerate((k_hbm, v_hbm)):

            @pl.when(a_does)
            def _():
                copy(OWN_A, ref, N2, head, kv, at(seg, x + 1, core)).start()

            @pl.when(b_does)
            def _():
                copy(OWN_B, ref, N4, head, kv, at(seg, x + 2, core)).start()

        return carry

    def send_over(head, carry):
        for kv, ref in enumerate((k_hbm, v_hbm)):

            @pl.when(crosses)
            def _():
                copy(CROSSES, ref, c_slot, head, kv, c_dst).start()

        return carry

    def pass_on(head, carry):
        for kv in range(2):

            @pl.when(passes)
            def _():
                arrived(PASS, head, kv)
                copy(PASSED, slot.at[PASS, kv], x_slot, head, kv, p_dst).start()

        return carry

    lax.fori_loop(0, head_count, send_over, 0)
    lax.fori_loop(0, head_count, send_sibling, 0)
    lax.fori_loop(0, head_count, pass_on, 0)
    for number in range(4):

        @pl.when(ctx < number + 1)
        def _():
            slot[number] = jnp.zeros(slot.shape[1:], slot.dtype)

    for one in loads[:3]:
        one.wait()

    def w_copy(number, send_sem, device):
        rows_of = region_rows(number)
        return remote(wc.at[:, rows_of], wc.at[:, rows_of], send_sem, w_recv.at[number], device)

    def x_stage():
        @pl.when(there(mine))
        def _():
            def wait(step, carry):
                z_arrival(lax.rem(me + step, n)).wait_recv()
                return carry

            lax.fori_loop(1, n, wait, 0)

            def start(step, carry):
                w_copy(mine, x_send.at[step], at(seg, lax.rem(x + step, 4), core)).start()
                return carry

            lax.fori_loop(1, 4, start, 0)

    def y_stage():
        def one(x_of, carry):
            number = region(y, x_of, core)

            @pl.when(there(number) & (x_of != x))
            def _():
                w_copy(number, x_send.at[0], sibling).wait_recv()

            if y_count > 1:

                @pl.when(there(number))
                def _():
                    def start(step, carry):
                        w_copy(number, y_send.at[x_of, step], y_at(step)).start()
                        return carry

                    lax.fori_loop(1, y_count, start, 0)

            return carry

        lax.fori_loop(0, 4, one, 0)

    def each_lane_region(core_of, do):
        def one(index, carry):
            y_of, x_of = lax.div(index, 4), lax.rem(index, 4)
            number = region(y_of, x_of, core_of)

            @pl.when(there(number))
            def _():
                do(number, y_of)

            return carry

        lax.fori_loop(0, 4 * y_count, one, 0)

    def c_stage():
        def hand_over(number, y_of):
            @pl.when(y_of != y)
            def _():
                w_copy(number, x_send.at[0], sibling).wait_recv()

            w_copy(number, c_send.at[number], sibling).start()

        each_lane_region(core, hand_over)

    def c_arrivals():
        def wait(number, y_of):
            w_copy(number, c_send.at[number], sibling).wait_recv()

        each_lane_region(1 - core, wait)

    def w_sent():
        @pl.when(there(mine))
        def _():
            def z_wait(step, carry):
                z_copy(lax.rem(me + step, n)).wait_send()
                return carry

            lax.fori_loop(1, n, z_wait, 0)

            def x_wait(step, carry):
                w_copy(mine, x_send.at[step], sibling).wait_send()
                return carry

            lax.fori_loop(1, 4, x_wait, 0)

        def y_wait(x_of, carry):
            number = region(y, x_of, core)

            @pl.when(there(number))
            def _():
                def wait(step, carry):
                    w_copy(number, y_send.at[x_of, step], sibling).wait_send()
                    return carry

                lax.fori_loop(1, y_count, wait, 0)

            return carry

        if y_count > 1:
            lax.fori_loop(0, 4, y_wait, 0)
        each_lane_region(core, lambda number, y_of: w_copy(number, c_send.at[number], sibling).wait_send())

    query_at = lax.broadcasted_iota(jnp.int32, (1, rows), 1)
    start = jnp.zeros((1, rows), jnp.int32)
    end = 0
    for doc in range(docs_ref.shape[0]):
        end = end + docs_ref[doc]
        start = jnp.where(end <= query_at + first_pos, end, start)
    start = start - first_pos
    key_at = lax.broadcasted_iota(jnp.int32, (rows, rows), 0)

    extra_row = lax.broadcasted_iota(jnp.int32, (EXTRA, rows), 0)
    extra_col = lax.broadcasted_iota(jnp.int32, (EXTRA, rows), 1)

    def key_rows(number):
        low = lax.rem(extra_col, 16)
        high = extra_col - low - (number + 1) * rows
        ones = jnp.where(extra_row < 9, 1, 0)
        picked = jnp.where(extra_row < 3, high, jnp.where(extra_row < 6, low, ones))
        return picked.astype(jnp.float32).astype(jnp.bfloat16)

    def prepare(head, carry):
        base = (me * head_count + head) * 4
        whole = slopes_ref[base]
        here = part_of(q_ref, head)[...].astype(jnp.float32) * (LOG2E / math.sqrt(HD))
        high = here.astype(jnp.bfloat16)
        low = (here - high.astype(jnp.float32)).astype(jnp.bfloat16)
        shift = -whole * extra_col.astype(jnp.float32)
        shift_1 = shift.astype(jnp.bfloat16).astype(jnp.float32)
        shift_2 = (shift - shift_1).astype(jnp.bfloat16).astype(jnp.float32)
        shift_3 = shift - shift_1 - shift_2
        which = lax.rem(extra_row, 3)
        slope = jnp.where(
            which == 0, slopes_ref[base + 1], jnp.where(which == 1, slopes_ref[base + 2], slopes_ref[base + 3])
        )
        moved = jnp.where(which == 0, shift_1, jnp.where(which == 1, shift_2, shift_3))
        rows_of = jnp.where(extra_row < 6, slope, jnp.where(extra_row < 9, moved, 0.0))
        qx[head, pl.ds(0, HD)] = high
        qx[head, pl.ds(HD, EXTRA)] = rows_of.astype(jnp.bfloat16)
        qx[head, pl.ds(HD + EXTRA, HD)] = low
        qx[head, pl.ds(2 * HD + EXTRA, EXTRA)] = jnp.zeros((EXTRA, rows), jnp.bfloat16)
        return carry

    lax.fori_loop(0, head_count, prepare, 0)

    def score(keys, number, head):
        keys = jnp.concatenate([keys, key_rows(number)], axis=0)
        keys = jnp.transpose(keys)
        keys = jnp.concatenate([keys, keys], axis=1)
        return jnp.dot(keys, qx[head], preferred_element_type=jnp.float32)

    def own_block(head, carry):
        found = score(part_of(own.at[0], head)[...], -1, head)
        allowed = (key_at <= query_at) & (key_at >= start)
        found = jnp.where(allowed, found, NEVER)
        most = jnp.max(found, axis=0, keepdims=True)
        weights = jnp.exp2(found - most)
        total[head] = jnp.sum(weights, axis=0, keepdims=True)
        top[head] = most
        part_of(acc, head)[...] = jnp.dot(
            part_of(own.at[1], head)[...], weights.astype(jnp.bfloat16), preferred_element_type=jnp.float32
        )
        return carry

    lax.fori_loop(0, head_count, send_own, 0)
    loads[3].wait()
    lax.fori_loop(0, n // 2, transpose_pair, 0)

    @pl.when(there(mine))
    def _():
        wc[me, region_rows(mine)] = wt[me, region_rows(mine)]

        def start(step, carry):
            z_copy(lax.rem(me + step, n)).start()
            return carry

        lax.fori_loop(1, n, start, 0)

    lax.fori_loop(0, head_count // 2, own_block, 0)
    lax.fori_loop(head_count // 2, head_count, own_block, 0)

    def hand_on(head, carry):
        for kv in range(2):
            arrived(N2, head, kv)
            copy(SECOND, slot.at[N2, kv], N4, head, kv, at(seg, 2, core)).start()
        return carry

    @pl.when(x == 1)
    def _():
        lax.fori_loop(0, head_count, hand_on, 0)

    def hand_out(head, kv):
        @pl.when((ctx >= 2) & (x != 1))
        def _():
            arrived(N2, head, kv)

        @pl.when((x == 0) & has_prev)
        def _():
            copy(SECOND, slot.at[N2, kv], N4, head, kv, at(seg, 1, core)).start()

        @pl.when(ctx >= 2)
        def _():
            copy(SIB_N2, slot.at[N2, kv], jnp.where(core == 0, N3, N1), head, kv, sibling).start()

    def bring(head, kv):
        @pl.when(ctx >= 4)
        def _():
            arrived(N4, head, kv)

        @pl.when((ctx >= 4) & (core == 1))
        def _():
            copy(SIB_N4, slot.at[N4, kv], N3, head, kv, sibling).start()

        @pl.when(ctx >= 1)
        def _():
            arrived(N1, head, kv)

        @pl.when(ctx >= 3)
        def _():
            arrived(N3, head, kv)

    def earlier_blocks(head, carry):
        hand_out(head, 0)
        hand_out(head, 1)
        bring(head, 0)
        most = top[head]
        for number in range(4):
            found = score(part_of(slot.at[number, 0], head)[...], number, head)
            found = jnp.where(key_at >= start + (number + 1) * rows, found, NEVER)
            scores[number] = found
            most = jnp.maximum(most, jnp.max(found, axis=0, keepdims=True))
        factor = jnp.exp2(top[head] - most)
        added = total[head] * factor
        for number in range(4):
            weights = jnp.exp2(scores[number] - most)
            added = added + jnp.sum(weights, axis=0, keepdims=True)
            probs[number] = weights.astype(jnp.bfloat16)
        bring(head, 1)

        summed = part_of(acc, head)[...] * factor
        for number in range(4):
            summed = summed + jnp.dot(
                part_of(slot.at[number, 1], head)[...], probs[number], preferred_element_type=jnp.float32
            )
        attended = (summed / added).astype(jnp.bfloat16)
        part_of(first_half, head)[...] = attended[:, : 2 * piece_len]
        for piece in range(2):
            part_of(spread.at[me, piece], head)[...] = attended[:, (2 + piece) * piece_len : (3 + piece) * piece_len]

        return carry

    lax.fori_loop(0, head_count, earlier_blocks, 0)

    places = ((ctx, me + 1), (ctx, me - 1))
    below = (me, n - 1 - me)

    def spread_copy(way, source, piece):
        ref = spread.at[source, piece]
        return remote(ref, ref, spread_send.at[way, source, piece], spread_recv.at[source, piece], places[way])

    def part_copy(way, owner, piece):
        return remote(
            part.at[owner, piece],
            came.at[way, owner, piece],
            part_send.at[owner, piece],
            part_recv.at[way, owner, piece],
            places[way],
        )

    for piece in range(2):
        for way in (UP, DOWN):

            @pl.when(below[way] < n - 1)
            def _():
                spread_copy(way, me, piece).start()

    x_stage()

    def partials(owner, carry):
        found = jnp.dot(wt[owner, :, :cols], first_half[...], preferred_element_type=jnp.float32).astype(jnp.bfloat16)
        for piece in range(2):
            part[owner, piece] = found[:, piece * piece_len : (piece + 1) * piece_len]
        return carry

    lax.fori_loop(0, n, partials, 0)
    for piece in range(2):
        second_half[piece] = jnp.dot(wt[me, :, :cols], spread[me, piece], preferred_element_type=jnp.float32)
    def slot_of(time, carry):
        number, piece = lax.div(time, 2), lax.rem(time, 2)
        for way in (UP, DOWN):
            behind = below[way]
            sign = 1 - 2 * way
            source = me - sign * number

            @pl.when(number <= behind)
            def _():
                spread_copy(way, source, piece).wait_recv()

            @pl.when((number <= behind) & (behind < n - 1))
            def _():
                spread_copy(way, source, piece).start()

            owner = jnp.where(way == UP, n - 1, 0) - sign * (number - behind - 1)
            sums = (number > behind) & (behind < n - 1)

            @pl.when(sums & (behind > 0))
            def _():
                part_copy(way, owner, piece).wait_recv()
                summed = part[owner, piece].astype(jnp.float32) + came[way, owner, piece].astype(jnp.float32)
                part[owner, piece] = summed.astype(jnp.bfloat16)

            @pl.when(sums)
            def _():
                part_copy(way, owner, piece).start()

        return carry

    lag = min(4, 2 * n - 2)

    def product(time, carry):
        number, piece = lax.div(time, 2), lax.rem(time, 2)
        for way in (UP, DOWN):
            source = me - (1 - 2 * way) * number

            @pl.when(number <= below[way])
            def _():
                second_half[piece] += jnp.dot(
                    wc[source, :, :cols], spread[source, piece], preferred_element_type=jnp.float32
                )

        return carry

    soon = min(6, 2 * n)
    late = max(soon, 2 * n - 2)
    lax.fori_loop(2, soon, slot_of, 0)
    y_stage()
    lax.fori_loop(soon, late, slot_of, 0)
    c_stage()
    lax.fori_loop(late, 2 * n, slot_of, 0)
    c_arrivals()
    lax.fori_loop(2, 2 * n, product, 0)
    for piece in range(2):
        for way in (UP, DOWN):

            @pl.when(below[way] > 0)
            def _():
                part_copy(way, me, piece).wait_recv()

        whole = part[me, piece].astype(jnp.float32)
        for way in (UP, DOWN):
            whole = whole + jnp.where(below[way] > 0, came[way, me, piece].astype(jnp.float32), 0.0)
        o_ref[:, piece * piece_len : (piece + 1) * piece_len] = whole.astype(jnp.bfloat16)
        o_ref[:, (2 + piece) * piece_len : (3 + piece) * piece_len] = second_half[piece].astype(jnp.bfloat16)

    def sent(head, carry):
        for kv, ref in enumerate((k_hbm, v_hbm)):
            for what, does in (
                (OWN_A, a_does),
                (OWN_B, b_does),
                (CROSSES, crosses),
                (PASSED, passes),
                (SECOND, second),
                (SIB_OWN, core == 0),
                (SIB_N2, ctx >= 2),
                (SIB_N4, (ctx >= 4) & (core == 1)),
            ):

                @pl.when(does)
                def _():
                    copy(what, ref, N1, head, kv, sibling).wait_send()

        return carry

    lax.fori_loop(0, head_count, sent, 0)
    w_sent()

    def sums_sent(other, carry):
        for piece in range(2):

            @pl.when(other != me)
            def _():
                part_copy(UP, other, piece).wait_send()

            for way in (UP, DOWN):
                sign = 1 - 2 * way
                passed = (below[way] < n - 1) & ((me - other) * sign >= 0)

                @pl.when(passed)
                def _():
                    spread_copy(way, other, piece).wait_send()

        return carry

    lax.fori_loop(0, n, sums_sent, 0)


def layer(doc_lengths, slopes, queries, keys, values, out_weight):
    cols, rows = queries.shape
    heads = cols // HD
    n = out_weight.shape[1] // cols
    y_count = max(1, lax.axis_size("ctx") // 16)
    regions = 8 * y_count
    piece = rows // PIECES
    lanes = 128 * -(-cols // 128)
    bf16, f32 = jnp.bfloat16, jnp.float32
    vmem, smem = pl.BlockSpec(memory_space=pltpu.VMEM), pl.BlockSpec(memory_space=pltpu.SMEM)
    anywhere = pl.BlockSpec(memory_space=pl.ANY)
    dma = pltpu.SemaphoreType.DMA
    return pl.pallas_call(
        layer_kernel,
        out_shape=jax.ShapeDtypeStruct((cols, rows), bf16),
        in_specs=[smem, smem, anywhere, anywhere, anywhere, anywhere],
        out_specs=vmem,
        scratch_shapes=[
            pltpu.VMEM((cols, rows), bf16),
            pltpu.VMEM((2, cols, rows), bf16),
            pltpu.VMEM((cols, n * cols), bf16),
            pltpu.VMEM((5, 2, cols, rows), bf16),
            pltpu.VMEM((heads, 2 * (HD + EXTRA), rows), bf16),
            pltpu.VMEM((4, rows, rows), f32),
            pltpu.VMEM((4, rows, rows), bf16),
            pltpu.VMEM((cols, rows), f32),
            pltpu.VMEM((heads, 1, rows), f32),
            pltpu.VMEM((heads, 1, rows), f32),
            pltpu.VMEM((n, cols, lanes), bf16),
            pltpu.VMEM((n, cols, lanes), bf16),
            pltpu.VMEM((cols, 2 * piece), bf16),
            pltpu.VMEM((n, 2, cols, piece), bf16),
            pltpu.VMEM((n, 2, cols, piece), bf16),
            pltpu.VMEM((2, n, 2, cols, piece), bf16),
            pltpu.VMEM((2, cols, piece), f32),
            dma((4,)),
            dma((8, 2, heads)),
            dma((5, 2, heads)),
            dma((n,)),
            dma((n,)),
            dma((4,)),
            dma((4, y_count)),
            dma((regions,)),
            dma((regions,)),
            dma((2, n, 2)),
            dma((n, 2)),
            dma((n, 2)),
            dma((2, n, 2)),
        ],
        compiler_params=pltpu.CompilerParams(
            collective_id=0, has_side_effects=True, vmem_limit_bytes=56 << 20
        ),
    )(doc_lengths, slopes, queries, keys, values, out_weight)


def body(queries, keys, values, out_weight, doc_lengths):
    all_heads = queries.shape[1] // HD * lax.axis_size("tp")
    slopes = jnp.asarray(slope_table(all_heads))
    return layer(doc_lengths, slopes, queries.T, keys.T, values.T, out_weight).T


def solution(mesh):
    placed = (P("ctx", "tp"), P("ctx", "tp"), P("ctx", "tp"), P("tp", None), P())
    return jax.shard_map(
        body, mesh=mesh, in_specs=placed, out_specs=P("ctx", "tp"), check_vma=False
    )
```
